32 devices in a mesh: scen: 2 (over y), slab: 4 (over z), section: 2 (over x), pencil: 2 (over core).
Axes of the slice: x: 2, y: 2, z: 4, core: 2. Of those that a mesh axis runs over, the one named last changes fastest.
Arguments:
- checkpoint_state: float32 [5, 64, 16, 128], P(None, ('scen', 'slab', 'section'), 'pencil'), parts along dimension 1, may hold values from -6 to 6
- start_state: float32 [5, 64, 16, 128], P(None, ('scen', 'slab', 'section'), 'pencil'), parts along dimension 1, may hold values from -6 to 6
- target_temp: float32 [64, 16, 128], P(('scen', 'slab', 'section'), 'pencil'), parts along dimension 0, may hold values from -6 to 6
- zone_map: int32 [64, 16, 128], P(('scen', 'slab', 'section'), 'pencil'), parts along dimension 0, may hold values from 0 to 63, as said below
- controls_now: float32 [8, 64], P('scen'), parts along dimension 0, may hold values from -6 to 6
- controls_next: float32 [8, 64], P('scen'), parts along dimension 0, may hold values from -6 to 6
- heat_gain: float32 [64], replicated, may hold values from 0.05 to 0.3
- diffusivity: float32 [5], replicated, may hold values from 0.03 to 0.15
- coupling: float32 [5, 5], replicated, may hold values from -0.05 to 0.05
Outputs:
- end_state: float32 [5, 64, 16, 128], P(None, ('scen', 'slab', 'section'), 'pencil'), parts along dimension 1
- control_grad: float32 [8, 64], P('scen', ('slab', 'section', 'pencil')), parts along dimension 0
The draws below stay inside these ranges and needn't reach their ends.
There are 2 independent parts, one for each index of `scen`. The reference program is written for one: setup_inputs(seed, part) draws one part's arguments, and reference() takes and returns one part's arrays. A program takes and returns all parts, laid end to end along the dimension named above; an argument that names none is the same for every part. Nothing has to cross between parts.
Inputs may be any that keep to these rules, and one draw needn't show every extreme that they name: `zone_map`: each zone is the cells of one box, 8 cells along the first dimension and 8 along the second, with borders along the third dimension that vary from box to box; every zone holds at least one cell and every zone number occurs.
All inputs are finite; a program needn't handle non-finite values.
Results may differ from the reference program's by a relative error of at most 0.0001.
Values sent between devices are 32-bit elements; how exact they have to be, the bound alone decides.
A program may use at most 64 MiB of HBM per device.

```python
import math
import jax
import jax.numpy as jnp

F = 5
K = 4
CX = 8
CY = 8
NX = 32
NY = 16
NZ = 128
ZONES = 64
CELLS_ZONE = 1024


def draw_zone_map(key, part):
    xboxes = NX // CX
    yboxes = NY // CY
    pieces = ZONES // (xboxes * yboxes)
    length = NZ // pieces
    reach = length // 4
    jitter = jax.random.randint(jax.random.fold_in(key, 11), (xboxes, yboxes, max(pieces - 1, 1)), -reach, reach + 1).astype(jnp.int32)
    bounds = (jnp.arange(1, pieces, dtype=jnp.int32) * length)[None, None, :] + jitter[:, :, :pieces - 1]
    depth = jnp.arange(NZ, dtype=jnp.int32)
    piece = jnp.sum((depth[None, None, :, None] >= bounds[:, :, None, :]).astype(jnp.int32), axis=-1).astype(jnp.int32)
    boxes = jnp.arange(xboxes, dtype=jnp.int32)[:, None] * yboxes + jnp.arange(yboxes, dtype=jnp.int32)[None, :]
    local = boxes[:, :, None] * pieces + piece
    order = jax.random.permutation(jax.random.fold_in(key, 12), ZONES).astype(jnp.int32)
    labels = order[local]
    spread = jnp.broadcast_to(labels[:, None, :, None, :], (xboxes, CX, yboxes, CY, NZ))
    return spread.reshape((NX, NY, NZ)).astype(jnp.int32)


def block_levels(own_key, dims, shards, smallest, high):
    def one(position, shards_of):
        heights = jax.random.uniform(jax.random.fold_in(jax.random.fold_in(own_key, 6), position), (shards_of,), jnp.float32, smallest / len(shards), high / len(shards))
        return jnp.repeat(jnp.exp(heights), dims[position] // shards_of).reshape((-1,) + (1,) * (len(dims) - position - 1))

    factor_of = one(*shards[0])
    for cut in shards[1:]:
        factor_of = factor_of * one(*cut)
    return factor_of


def normal_values(key, dims, deviation, bound, cuts=(), kind=jnp.bfloat16):
    array = deviation * jax.random.normal(key, dims, jnp.float32)
    if cuts:
        array = array * block_levels(key, dims, cuts, -0.22, 0.18)
    return jnp.clip(array, -bound, bound).astype(kind)


def setup_inputs(seed: int = 0, part: int = 0) -> dict:
    splits = jax.random.split(jax.random.key(seed), 10)
    part_splits = jax.random.split(jax.random.fold_in(splits[9], part), 10)
    checkpoint_state = normal_values(part_splits[0], (F, NX, NY, NZ), 1.0, 6.0, ((1, 8), (2, 2)), jnp.float32)
    start_state = normal_values(part_splits[1], (F, NX, NY, NZ), 1.0, 6.0, ((1, 8), (2, 2)), jnp.float32)
    target_temp = normal_values(part_splits[2], (NX, NY, NZ), 1.0, 6.0, ((0, 8), (1, 2)), jnp.float32)
    zone_map = draw_zone_map(jax.random.fold_in(jax.random.fold_in(splits[9], part), 71), part)
    controls_now = normal_values(part_splits[4], (K, ZONES), 1.0, 6.0, (), jnp.float32)
    controls_next = normal_values(part_splits[5], (K, ZONES), 1.0, 6.0, (), jnp.float32)
    heat_gain = jnp.clip(jnp.exp(jax.random.uniform(splits[6], (ZONES,), jnp.float32, math.log(0.05), math.log(0.3))), 0.05, 0.3)
    diffusivity = jnp.clip(jnp.exp(jax.random.uniform(splits[7], (F,), jnp.float32, math.log(0.03), math.log(0.15))), 0.03, 0.15)
    coupling = jnp.clip(jax.random.uniform(splits[8], (F, F), jnp.float32, -0.05, 0.05), -0.05, 0.05)
    return {"checkpoint_state": checkpoint_state, "start_state": start_state, "target_temp": target_temp, "zone_map": zone_map, "controls_now": controls_now, "controls_next": controls_next, "heat_gain": heat_gain, "diffusivity": diffusivity, "coupling": coupling}


def stencil_advance(current, diffusivity, coupling, injected):
    padded = jnp.pad(current, ((0, 0), (1, 1), (1, 1), (1, 1)))
    beside = padded[:, 2:, 1:-1, 1:-1] + padded[:, :-2, 1:-1, 1:-1]
    beside = beside + padded[:, 1:-1, 2:, 1:-1] + padded[:, 1:-1, :-2, 1:-1]
    beside = beside + padded[:, 1:-1, 1:-1, 2:] + padded[:, 1:-1, 1:-1, :-2]
    coupled = coupling[:, 0, None, None, None] * current[0:1]
    for source in range(1, current.shape[0]):
        coupled = coupled + coupling[:, source, None, None, None] * current[source:source + 1]
    updated = current + diffusivity[:, None, None, None] * (beside - 6.0 * current) + coupled
    return updated.at[0].add(injected)

def tracking_loss(controls_now, checkpoint_state, target_temp, zone_map, heat_gain, diffusivity, coupling):
    heat_table = heat_gain[None, :] * controls_now
    advance = jax.checkpoint(stencil_advance)
    current = checkpoint_state
    total = jnp.zeros((), jnp.float32)
    for step_index in range(K):
        current = advance(current, diffusivity, coupling, heat_table[step_index][zone_map])
        misfit = current[0] - target_temp
        total = total + 0.5 * jnp.sum(misfit * misfit)
    return total

def reference(checkpoint_state, start_state, target_temp, zone_map, controls_now, controls_next, heat_gain, diffusivity, coupling):
    gradient = jax.grad(tracking_loss)(controls_now, checkpoint_state, target_temp, zone_map, heat_gain, diffusivity, coupling)
    control_grad = gradient / math.sqrt(CELLS_ZONE)
    next_table = heat_gain[None, :] * controls_next
    current = start_state
    for step_index in range(K):
        current = stencil_advance(current, diffusivity, coupling, next_table[step_index][zone_map])
    return (current, control_grad)
```

```python
import functools
import math

import jax
import jax.numpy as jnp
import numpy as np
from jax import lax
from jax.experimental import pallas as pl
from jax.experimental.pallas import tpu as pltpu
from jax.sharding import PartitionSpec as P

CELLS_ZONE = 1024
BOX = 8
HIGHEST = lax.Precision.HIGHEST
MESH = pl.DeviceIdType.MESH


def laplacian_1d(n):
    return -2.0 * np.eye(n) + np.eye(n, k=1) + np.eye(n, k=-1)


def geometry(nx, ny, depth, pencils, steps):
    rows = ny // pencils
    phases = BOX // depth
    lx, ly = laplacian_1d(nx), laplacian_1d(ny)
    boxes = nx // BOX

    def powers(bx, by):
        field = np.zeros((nx, ny))
        if 0 <= bx < boxes:
            field[bx * BOX : (bx + 1) * BOX, by * BOX : (by + 1) * BOX] = 1.0
        out = []
        for _ in range(steps):
            out.append(field)
            field = lx @ field + field @ ly.T
        return out

    table = np.zeros((phases * 3 * pencils, steps * 4, steps * depth * rows), np.float32)
    for phase in range(phases):
        side = -1 if 2 * phase < phases else 1
        for edge, bx in enumerate((0, boxes // 2, boxes - 1)):
            x0 = bx * BOX + phase * depth
            for pencil in range(pencils):
                for xb in range(2):
                    for yb in range(2):
                        fields = powers(bx + side * xb, pencil if yb == 0 else 1 - pencil)
                        for r in range(steps):
                            block = fields[r][x0 : x0 + depth, pencil * rows : (pencil + 1) * rows]
                            table[(phase * 3 + edge) * pencils + pencil, r * 4 + xb * 2 + yb] = (
                                np.tile(block.reshape(-1), steps)
                            )
    return table


def kernel(
    cfg,
    check_ref,
    start_ref,
    target_ref,
    zone_ref,
    now_ref,
    next_ref,
    gain_ref,
    diff_ref,
    coup_ref,
    geo_ref,
    end_ref,
    grad_ref,
    halo,
    zhalo,
    qbuf,
    sums,
    got,
    halo_send,
    halo_recv,
    sum_send,
    sum_recv,
):
    nslab, nsec, npen, F, depth, NZ, K, zones = cfg
    nline = nslab * nsec
    count = nline * npen
    own = zones // count
    hops = -(-K // depth)
    phases = BOX // depth
    pencil = lax.axis_index("pencil")
    line = lax.axis_index("slab") * nsec + lax.axis_index("section")
    me = line * npen + pencil

    def where_is(at, pen):
        return {"slab": at // nsec, "section": at % nsec, "pencil": pen}

    slots = {}
    for off in range(-hops, hops + 1):
        for other in range(2):
            if (off, other) != (0, 0):
                slots[(off, other)] = len(slots)
    nslots = len(slots)

    barrier = pltpu.get_barrier_semaphore()

    def greet(r, carry):
        peer = lax.rem(me + r, count)
        pl.semaphore_signal(
            barrier, inc=1, device_id=where_is(peer // npen, peer % npen), device_id_type=MESH
        )
        return carry

    lax.fori_loop(1, count, greet, 0)
    pl.semaphore_wait(barrier, count - 1)

    pieces = (
        (zone_ref.at[0], lambda slot: zhalo.at[slot]),
        (check_ref, lambda slot: halo.at[0, slot]),
        (start_ref, lambda slot: halo.at[1, slot]),
    )

    def copy_to(what, off, other, arriving):
        here = slots[(off, other)]
        slot = here if arriving else slots[(-off, other)]
        src, dst = pieces[what]
        return pltpu.make_async_remote_copy(
            src_ref=src,
            dst_ref=dst(slot),
            send_sem=halo_send.at[what, here],
            recv_sem=halo_recv.at[what, slot],
            device_id=where_is(line + off, pencil if other == 0 else 1 - pencil),
            device_id_type=MESH,
        )

    def exists(off):
        return jnp.logical_and(line + off >= 0, line + off < nline)

    for what in range(3):
        for off, other in slots:

            @pl.when(exists(off))
            def _(off=off, other=other, what=what):
                copy_to(what, off, other, False).start()

    for off, other in slots:
        if off != 0:
            slot = slots[(off, other)]

            @pl.when(jnp.logical_not(exists(off)))
            def _(slot=slot):
                halo[0, slot] = jnp.zeros_like(halo[0, slot])
                halo[1, slot] = jnp.zeros_like(halo[1, slot])
                zhalo[slot] = jnp.zeros_like(zhalo[slot])

    diff = [diff_ref[f] for f in range(F)]
    coup = [[coup_ref[f, g] for g in range(F)] for f in range(F)]
    mix = [
        [coup[f][g] + (1.0 - 6.0 * diff[f]) if f == g else coup[f][g] for g in range(F)]
        for f in range(F)
    ]
    alpha = {(0, 0): jnp.float32(1.0)}
    rows = {0: [jnp.float32(1.0) if f == 0 else None for f in range(F)]}
    for p in range(1, K):
        new = {}
        for q in range(p + 1):
            vec = []
            for g in range(F):
                total = None
                if q in rows:
                    for f in range(F):
                        v = rows[q][f]
                        if v is not None:
                            c = coup[f][g] + 1.0 if f == g else coup[f][g]
                            total = v * c if total is None else total + v * c
                if q - 1 in rows and rows[q - 1][g] is not None:
                    v = rows[q - 1][g] * diff[g]
                    total = v if total is None else total + v
                vec.append(total)
            new[q] = vec
        rows = new
        for q in range(p + 1):
            alpha[(p, q)] = rows[q][0]

    lanes = K * depth * BOX
    wide = K * own
    shape = (wide, lanes)
    age = (
        lax.broadcasted_iota(jnp.int32, shape, 1) // (depth * BOX)
        - lax.broadcasted_iota(jnp.int32, shape, 0) // own
    )
    poly = []
    for q in range(K):
        part = jnp.zeros(shape, jnp.float32)
        for p in range(q, K):
            part = jnp.where(age == p, alpha[(p, q)], part)
        poly.append(part)
    phase = line % phases
    edge = jnp.where(line < phases, 0, jnp.where(line >= nline - phases, 2, 1))
    geo = geo_ref[(phase * 3 + edge) * npen + pencil]
    weights = []
    for c in range(K):
        for box in range(4):
            total = None
            for r in range(K - c):
                term = (math.comb(r + c, c) * poly[r + c]) * geo[r * 4 + box : r * 4 + box + 1]
                total = term if total is None else total + term
            weights.append(total)
    weights = jnp.concatenate(weights, axis=0)

    lane = lax.broadcasted_iota(jnp.int32, (BOX, NZ), 1)
    row = lax.broadcasted_iota(jnp.int32, (BOX, NZ), 0)
    not_first, not_last = lane > 0, lane < NZ - 1
    top, bottom = row == BOX - 1, row == 0
    half = BOX // 2
    beyond = row // half == pencil

    def along_z(v):
        low = jnp.where(not_first[: v.shape[0]], pltpu.roll(v, 1, 1), 0.0)
        high = jnp.where(not_last[: v.shape[0]], pltpu.roll(v, NZ - 1, 1), 0.0)
        return low + high

    gain = gain_ref[...].reshape(1, zones)
    tables = jnp.concatenate(
        [
            now_ref[...] * gain,
            next_ref[...] * gain,
            jnp.broadcast_to(gain * (1.0 / math.sqrt(CELLS_ZONE)), (BOX, zones)),
        ],
        axis=0,
    )

    def inject(zrow, slot):
        zone = lax.broadcasted_iota(jnp.int32, (zones, NZ), 0)
        hot = (zone == jnp.broadcast_to(zrow, (zones, NZ))).astype(jnp.float32)
        qbuf[slot] = jnp.dot(tables, hot, precision=HIGHEST, preferred_element_type=jnp.float32)

    inject(zone_ref[0][0:1], nslots)

    for off, other in slots:

        @pl.when(exists(off))
        def _(off=off, other=other):
            copy = copy_to(0, off, other, True)
            copy.wait_send()
            copy.wait_recv()

    for off, other in slots:
        slot = slots[(off, other)]
        inject(zhalo[slot][0:1], slot)

    inside = {off: jnp.where(exists(off), 1.0, 0.0) for off in range(-hops, hops + 1)}

    def off_of(plane):
        return plane // depth

    def forward(which, ref, seen):
        def plane_of(f, plane, other):
            off = off_of(plane)
            if off == 0 and other == 0:
                return ref[f, plane]
            v = halo[which, slots[(off, other)], f, plane - off * depth]
            return jnp.where(beyond, v, 0.0) if other else v

        T = [{p: plane_of(f, p, 0) for p in range(-K, depth + K)} for f in range(F)]
        U = [{p: plane_of(f, p, 1) for p in range(1 - K, depth + K - 1)} for f in range(F)]
        for step in range(K):
            reach = K - 1 - step
            newT = [{} for _ in range(F)]
            newU = [{} for _ in range(F)]
            for p in range(-reach, depth + reach):
                off = off_of(p)
                both = -reach < p < depth + reach - 1
                qt = qbuf[nslots if off == 0 else slots[(off, 0)], which * K + step : which * K + step + 1]
                if both:
                    qu = qbuf[slots[(off, 1)], which * K + step : which * K + step + 1]
                for f in range(F):
                    t, u = T[f][p], U[f][p]
                    tu, td = pltpu.roll(t, BOX - 1, 0), pltpu.roll(t, 1, 0)
                    uu, ud = pltpu.roll(u, BOX - 1, 0), pltpu.roll(u, 1, 0)
                    beside = T[f][p - 1] + T[f][p + 1] + along_z(t)
                    beside = beside + jnp.where(top, uu, tu) + jnp.where(bottom, ud, td)
                    v = diff[f] * beside
                    for g in range(F):
                        v = v + mix[f][g] * T[g][p]
                    if f == 0:
                        v = v + qt
                    if off != 0:
                        v = v * inside[off]
                    newT[f][p] = v
                    if both:
                        beside = U[f][p - 1] + U[f][p + 1] + along_z(u)
                        beside = beside + jnp.where(top, tu, uu) + jnp.where(bottom, td, ud)
                        v = diff[f] * beside
                        for g in range(F):
                            v = v + mix[f][g] * U[g][p]
                        if f == 0:
                            v = v + qu
                        if off != 0:
                            v = v * inside[off]
                        newU[f][p] = jnp.where(beyond, v, 0.0)
            T, U = newT, newU
            seen(T)
        return T

    def wait_halo(what):
        for off, other in slots:

            @pl.when(exists(off))
            def _(off=off, other=other):
                copy = copy_to(what, off, other, True)
                copy.wait_send()
                copy.wait_recv()

    wait_halo(1)
    misfits = []

    def seen(T):
        for p in range(depth):
            misfits.append(T[0][p] - target_ref[p])

    forward(0, check_ref, seen)
    R = jnp.dot(
        weights,
        jnp.concatenate(misfits, axis=0),
        precision=HIGHEST,
        preferred_element_type=jnp.float32,
    )
    zlane = lax.broadcasted_iota(jnp.int32, (wide, NZ), 1)
    side = jnp.where(2 * phase < phases, -(phase + 1), phases - phase)
    lhs, rhs = [], []
    for box in range(4):
        acc = None
        for c in range(K - 1, -1, -1):
            part = R[(c * 4 + box) * wide : (c * 4 + box + 1) * wide]
            if acc is None:
                acc = part
            else:
                low = jnp.where(zlane > 0, pltpu.roll(acc, 1, 1), 0.0)
                high = jnp.where(zlane < NZ - 1, pltpu.roll(acc, NZ - 1, 1), 0.0)
                acc = part + (low + high - 2.0 * acc)
        xb, yb = box // 2, box % 2
        if xb == 0:
            slot = nslots if yb == 0 else slots[(0, 1)]
            zrow = zone_ref[0][0:1] if yb == 0 else zhalo[slot][0:1]
        else:
            slot = jnp.int32(0)
            for off in range(-hops, hops + 1):
                if off != 0:
                    slot = jnp.where(side == off, slots[(off, yb)], slot)
            zrow = zhalo[slot][0:1]
        rhs.append(acc * qbuf[slot][2 * K : 2 * K + 1])
        owner = lax.broadcasted_iota(jnp.int32, (own * count, NZ), 0)
        number = lax.rem(owner, count) * own + owner // count
        lhs.append((number == jnp.broadcast_to(zrow, number.shape)).astype(jnp.float32))
    S = None
    for a, b in zip(lhs, rhs):
        part = lax.dot_general(
            a, b, (((1,), (1,)), ((), ())), precision=HIGHEST, preferred_element_type=jnp.float32
        )
        S = part if S is None else S + part
    pick = lax.broadcasted_iota(jnp.int32, (count, wide), 1) % own
    mine = S[:count]
    for zz in range(1, own):
        mine = jnp.where(pick == zz, S[zz * count : (zz + 1) * count], mine)
    mine = jnp.concatenate([mine, jnp.zeros((count, 128 - wide), jnp.float32)], axis=1)
    for o in range(count):
        sums[o] = mine[o : o + 1]

    def give(r, carry):
        peer = lax.rem(me + r, count)
        pltpu.make_async_remote_copy(
            src_ref=sums.at[peer],
            dst_ref=got.at[r - 1],
            send_sem=sum_send,
            recv_sem=sum_recv,
            device_id=where_is(peer // npen, peer % npen),
            device_id_type=MESH,
        ).start()
        return carry

    lax.fori_loop(1, count, give, 0)

    wait_halo(2)
    T = forward(1, start_ref, lambda T: None)
    for f in range(F):
        for p in range(depth):
            end_ref[f, p] = T[f][p]

    pltpu.make_async_copy(got, got, sum_recv).wait()
    pltpu.make_async_copy(got, got, sum_send).wait()
    total = sums[me] + jnp.sum(got[...], axis=0)
    for k in range(K):
        grad_ref[k : k + 1, :] = total[:, k * own : (k + 1) * own]


def solution(mesh):
    nslab, nsec, npen = mesh.shape["slab"], mesh.shape["section"], mesh.shape["pencil"]

    def per_device(check, start, target, zone, now, nxt, gain, diff, coup):
        F, depth, rows, NZ = check.shape
        K, zones = now.shape
        nline = nslab * nsec
        count = nline * npen
        hops = -(-K // depth)
        nslots = 2 * (2 * hops + 1) - 1
        table = jnp.asarray(geometry(nline * depth, npen * rows, depth, npen, K))
        cfg = (nslab, nsec, npen, F, depth, NZ, K, zones)
        vmem = pl.BlockSpec(memory_space=pltpu.VMEM)
        smem = pl.BlockSpec(memory_space=pltpu.SMEM)
        return pl.pallas_call(
            functools.partial(kernel, cfg),
            out_shape=(
                jax.ShapeDtypeStruct(check.shape, jnp.float32),
                jax.ShapeDtypeStruct((K, zones // count), jnp.float32),
            ),
            in_specs=[vmem] * 7 + [smem] * 2 + [vmem],
            out_specs=(vmem, vmem),
            scratch_shapes=[
                pltpu.VMEM((2, nslots, F, depth, rows, NZ), jnp.float32),
                pltpu.VMEM((nslots, rows, NZ), jnp.int32),
                pltpu.VMEM((nslots + 1, 2 * K + 8, NZ), jnp.float32),
                pltpu.VMEM((count, 1, 128), jnp.float32),
                pltpu.VMEM((count - 1, 1, 128), jnp.float32),
                pltpu.SemaphoreType.DMA((3, nslots)),
                pltpu.SemaphoreType.DMA((3, nslots)),
                pltpu.SemaphoreType.DMA,
                pltpu.SemaphoreType.DMA,
            ],
            compiler_params=pltpu.CompilerParams(
                collective_id=0, has_side_effects=True, vmem_limit_bytes=32 * 1024 * 1024
            ),
        )(check, start, target, zone, now, nxt, gain, diff, coup, table)

    return jax.shard_map(
        per_device,
        mesh=mesh,
        in_specs=(
            P(None, ("scen", "slab", "section"), "pencil", None),
            P(None, ("scen", "slab", "section"), "pencil", None),
            P(("scen", "slab", "section"), "pencil", None),
            P(("scen", "slab", "section"), "pencil", None),
            P("scen", None),
            P("scen", None),
            P(),
            P(),
            P(),
        ),
        out_specs=(
            P(None, ("scen", "slab", "section"), "pencil", None),
            P("scen", ("slab", "section", "pencil")),
        ),
        check_vma=False,
    )
```

```python
import functools
import math

import jax
import jax.numpy as jnp
import numpy as np
from jax import lax
from jax.experimental import pallas as pl
from jax.experimental.pallas import tpu as pltpu
from jax.sharding import PartitionSpec as P

CELLS_ZONE = 1024
BOX = 8
HIGHEST = lax.Precision.HIGHEST
MESH = pl.DeviceIdType.MESH


def laplacian_1d(n):
    return -2.0 * np.eye(n) + np.eye(n, k=1) + np.eye(n, k=-1)


def geometry(nx, ny, depth, pencils, steps):
    rows = ny // pencils
    phases = BOX // depth
    lx, ly = laplacian_1d(nx), laplacian_1d(ny)
    boxes = nx // BOX

    def powers(bx, by):
        field = np.zeros((nx, ny))
        if 0 <= bx < boxes:
            field[bx * BOX : (bx + 1) * BOX, by * BOX : (by + 1) * BOX] = 1.0
        out = []
        for _ in range(steps):
            out.append(field)
            field = lx @ field + field @ ly.T
        return out

    table = np.zeros((phases * 3 * pencils, steps * 4, steps * depth * rows), np.float32)
    for phase in range(phases):
        side = -1 if 2 * phase < phases else 1
        for edge, bx in enumerate((0, boxes // 2, boxes - 1)):
            x0 = bx * BOX + phase * depth
            for pencil in range(pencils):
                for xb in range(2):
                    for yb in range(2):
                        fields = powers(bx + side * xb, pencil if yb == 0 else 1 - pencil)
                        for r in range(steps):
                            block = fields[r][x0 : x0 + depth, pencil * rows : (pencil + 1) * rows]
                            table[(phase * 3 + edge) * pencils + pencil, r * 4 + xb * 2 + yb] = (
                                np.tile(block.reshape(-1), steps)
                            )
    return table


def kernel(
    cfg,
    check_hbm,
    start_hbm,
    target_hbm,
    zone_hbm,
    now_hbm,
    next_hbm,
    gain_hbm,
    diff_hbm,
    coup_hbm,
    geo_hbm,
    end_ref,
    grad_ref,
    check_ref,
    start_ref,
    target_ref,
    zone_ref,
    now_ref,
    next_ref,
    gain_ref,
    diff_ref,
    coup_ref,
    geo_ref,
    packed,
    halo,
    corner,
    zhalo,
    qbuf,
    sums,
    got,
    load_sem,
    halo_send,
    halo_recv,
    sum_send,
    sum_recv,
):
    nslab, nsec, npen, F, depth, NZ, K, zones = cfg
    nline = nslab * nsec
    count = nline * npen
    own = zones // count
    hops = -(-K // depth)
    phases = BOX // depth
    pencil = lax.axis_index("pencil")
    line = lax.axis_index("slab") * nsec + lax.axis_index("section")
    me = line * npen + pencil
    phase = line % phases
    edge = jnp.where(line < phases, 0, jnp.where(line >= nline - phases, 2, 1))

    loads = [
        pltpu.make_async_copy(src, dst, load_sem.at[n])
        for n, (src, dst) in enumerate(
            (
                (check_hbm, check_ref),
                (start_hbm, start_ref),
                (coup_hbm, coup_ref),
                (diff_hbm, diff_ref),
                (geo_hbm.at[(phase * 3 + edge) * npen + pencil], geo_ref),
                (gain_hbm, gain_ref),
                (now_hbm, now_ref),
                (next_hbm, next_ref),
                (zone_hbm.at[0], zone_ref),
                (target_hbm, target_ref),
            )
        )
    ]
    for load in loads:
        load.start()

    def where_is(at, pen):
        return {"slab": at // nsec, "section": at % nsec, "pencil": pen}

    slots = {}
    for off in range(-hops, hops + 1):
        for other in range(2):
            if (off, other) != (0, 0):
                slots[(off, other)] = len(slots)
    nslots = len(slots)

    barrier = pltpu.get_barrier_semaphore()

    def greet(r, carry):
        peer = lax.rem(me + r, count)
        pl.semaphore_signal(
            barrier, inc=1, device_id=where_is(peer // npen, peer % npen), device_id_type=MESH
        )
        return carry

    lax.fori_loop(1, count, greet, 0)

    def exists(off):
        return jnp.logical_and(line + off >= 0, line + off < nline)

    for off, other in slots:
        if off != 0:
            slot = slots[(off, other)]

            @pl.when(jnp.logical_not(exists(off)))
            def _(slot=slot, other=other):
                for which in range(2):
                    if other:
                        corner[which, slot] = jnp.zeros_like(corner[which, slot])
                    else:
                        halo[which, slot] = jnp.zeros_like(halo[which, slot])
                zhalo[slot] = jnp.zeros_like(zhalo[slot])

    row = lax.broadcasted_iota(jnp.int32, (BOX, NZ), 0)

    def near(pen, at):
        return jnp.where(pen == 0, BOX - 1 - at, at)

    def turned(v, pen, back):
        first, second = (3, 5) if back else (5, 3)
        return jnp.where(pen == 0, pltpu.roll(v, first, 0), pltpu.roll(v, second, 0))

    near_1 = near(pencil, row) < 3
    near_2 = near(pencil, (row + 4) % BOX) < 2

    def plane_at(off, distance):
        plane = abs(off) * depth - distance
        plane = plane if off > 0 else depth - 1 - plane
        return plane if 0 <= plane < depth else None

    def pack(which, ref):
        for off in range(-hops, hops + 1):
            if off == 0:
                continue
            one, two, three = (plane_at(off, d) for d in (1, 2, 3))
            for f in range(F):
                tile = jnp.zeros((BOX, NZ), jnp.float32)
                if three is not None:
                    tile = turned(ref[f, three], pencil, False)
                if two is not None:
                    tile = jnp.where(near_2, pltpu.roll(ref[f, two], 4, 0), tile)
                if one is not None:
                    tile = jnp.where(near_1, ref[f, one], tile)
                packed[which, slots[(off, 1)], f] = tile

    loads[0].wait()
    pack(0, check_ref)
    loads[1].wait()
    pack(1, start_ref)
    pl.semaphore_wait(barrier, count - 1)

    def copy_to(what, off, other, arriving):
        here = slots[(off, other)]
        slot = here if arriving else slots[(-off, other)]
        if what == 0:
            src, dst = zone_hbm.at[0], zhalo.at[slot]
        elif off != 0 and other:
            src, dst = packed.at[what - 1, here], corner.at[what - 1, slot]
        else:
            src, dst = (check_hbm, start_hbm)[what - 1], halo.at[what - 1, slot]
        return pltpu.make_async_remote_copy(
            src_ref=src,
            dst_ref=dst,
            send_sem=halo_send.at[what, here],
            recv_sem=halo_recv.at[what, slot],
            device_id=where_is(line + off, pencil if other == 0 else 1 - pencil),
            device_id_type=MESH,
        )

    for what in range(3):
        for off, other in slots:

            @pl.when(exists(off))
            def _(off=off, other=other, what=what):
                copy_to(what, off, other, False).start()

    for load in loads[2:]:
        load.wait()

    diff = [diff_ref[f] for f in range(F)]
    coup = [[coup_ref[f, g] for g in range(F)] for f in range(F)]
    mix = [
        [coup[f][g] + (1.0 - 6.0 * diff[f]) if f == g else coup[f][g] for g in range(F)]
        for f in range(F)
    ]
    alpha = {(0, 0): jnp.float32(1.0)}
    rows = {0: [jnp.float32(1.0) if f == 0 else None for f in range(F)]}
    for p in range(1, K):
        new = {}
        for q in range(p + 1):
            vec = []
            for g in range(F):
                total = None
                if q in rows:
                    for f in range(F):
                        v = rows[q][f]
                        if v is not None:
                            c = coup[f][g] + 1.0 if f == g else coup[f][g]
                            total = v * c if total is None else total + v * c
                if q - 1 in rows and rows[q - 1][g] is not None:
                    v = rows[q - 1][g] * diff[g]
                    total = v if total is None else total + v
                vec.append(total)
            new[q] = vec
        rows = new
        for q in range(p + 1):
            alpha[(p, q)] = rows[q][0]

    lanes = K * depth * BOX
    wide = K * own
    shape = (wide, lanes)
    age = (
        lax.broadcasted_iota(jnp.int32, shape, 1) // (depth * BOX)
        - lax.broadcasted_iota(jnp.int32, shape, 0) // own
    )
    poly = []
    for q in range(K):
        part = jnp.zeros(shape, jnp.float32)
        for p in range(q, K):
            part = jnp.where(age == p, alpha[(p, q)], part)
        poly.append(part)
    geo = geo_ref[...]
    weights = []
    for c in range(K):
        for box in range(4):
            total = None
            for r in range(K - c):
                term = (math.comb(r + c, c) * poly[r + c]) * geo[r * 4 + box : r * 4 + box + 1]
                total = term if total is None else total + term
            weights.append(total)
    weights = jnp.concatenate(weights, axis=0)

    lane = lax.broadcasted_iota(jnp.int32, (BOX, NZ), 1)
    not_first, not_last = lane > 0, lane < NZ - 1
    top, bottom = row == BOX - 1, row == 0
    half = BOX // 2
    beyond = row // half == pencil

    def along_z(v):
        low = jnp.where(not_first[: v.shape[0]], pltpu.roll(v, 1, 1), 0.0)
        high = jnp.where(not_last[: v.shape[0]], pltpu.roll(v, NZ - 1, 1), 0.0)
        return low + high

    gain = gain_ref[...].reshape(1, zones)
    tables = jnp.concatenate(
        [
            now_ref[...] * gain,
            next_ref[...] * gain,
            jnp.broadcast_to(gain * (1.0 / math.sqrt(CELLS_ZONE)), (BOX, zones)),
        ],
        axis=0,
    )

    def inject(zrow, slot):
        zone = lax.broadcasted_iota(jnp.int32, (zones, NZ), 0)
        hot = (zone == jnp.broadcast_to(zrow, (zones, NZ))).astype(jnp.float32)
        qbuf[slot] = jnp.dot(tables, hot, precision=HIGHEST, preferred_element_type=jnp.float32)

    inject(zone_ref[0:1], nslots)

    for off, other in slots:

        @pl.when(exists(off))
        def _(off=off, other=other):
            copy = copy_to(0, off, other, True)
            copy.wait_send()
            copy.wait_recv()

    for off, other in slots:
        slot = slots[(off, other)]
        inject(zhalo[slot][0:1], slot)

    inside = {off: jnp.where(exists(off), 1.0, 0.0) for off in range(-hops, hops + 1)}

    def off_of(plane):
        return plane // depth

    def forward(which, ref, seen):
        def plane_of(f, plane, other):
            off = off_of(plane)
            if off == 0 and other == 0:
                return ref[f, plane]
            if off != 0 and other:
                v = corner[which, slots[(off, 1)], f]
                distance = -plane if off < 0 else plane - depth + 1
                if distance == 2:
                    v = pltpu.roll(v, 4, 0)
                if distance == 3:
                    v = turned(v, 1 - pencil, True)
                return jnp.where(near(1 - pencil, row) < K - distance, v, 0.0)
            v = halo[which, slots[(off, other)], f, plane - off * depth]
            return jnp.where(beyond, v, 0.0) if other else v

        T = [{p: plane_of(f, p, 0) for p in range(-K, depth + K)} for f in range(F)]
        U = [{p: plane_of(f, p, 1) for p in range(1 - K, depth + K - 1)} for f in range(F)]
        for step in range(K):
            reach = K - 1 - step
            newT = [{} for _ in range(F)]
            newU = [{} for _ in range(F)]
            for p in range(-reach, depth + reach):
                off = off_of(p)
                both = -reach < p < depth + reach - 1
                qt = qbuf[nslots if off == 0 else slots[(off, 0)], which * K + step : which * K + step + 1]
                if both:
                    qu = qbuf[slots[(off, 1)], which * K + step : which * K + step + 1]
                for f in range(F):
                    t, u = T[f][p], U[f][p]
                    tu, td = pltpu.roll(t, BOX - 1, 0), pltpu.roll(t, 1, 0)
                    uu, ud = pltpu.roll(u, BOX - 1, 0), pltpu.roll(u, 1, 0)
                    beside = T[f][p - 1] + T[f][p + 1] + along_z(t)
                    beside = beside + jnp.where(top, uu, tu) + jnp.where(bottom, ud, td)
                    v = diff[f] * beside
                    for g in range(F):
                        v = v + mix[f][g] * T[g][p]
                    if f == 0:
                        v = v + qt
                    if off != 0:
                        v = v * inside[off]
                    newT[f][p] = v
                    if both:
                        beside = U[f][p - 1] + U[f][p + 1] + along_z(u)
                        beside = beside + jnp.where(top, tu, uu) + jnp.where(bottom, td, ud)
                        v = diff[f] * beside
                        for g in range(F):
                            v = v + mix[f][g] * U[g][p]
                        if f == 0:
                            v = v + qu
                        if off != 0:
                            v = v * inside[off]
                        newU[f][p] = jnp.where(beyond, v, 0.0)
            T, U = newT, newU
            seen(T)
        return T

    def wait_halo(what):
        for off, other in slots:

            @pl.when(exists(off))
            def _(off=off, other=other):
                copy = copy_to(what, off, other, True)
                copy.wait_send()
                copy.wait_recv()

    wait_halo(1)
    misfits = []

    def seen(T):
        for p in range(depth):
            misfits.append(T[0][p] - target_ref[p])

    forward(0, check_ref, seen)
    R = jnp.dot(
        weights,
        jnp.concatenate(misfits, axis=0),
        precision=HIGHEST,
        preferred_element_type=jnp.float32,
    )
    zlane = lax.broadcasted_iota(jnp.int32, (wide, NZ), 1)
    side = jnp.where(2 * phase < phases, -(phase + 1), phases - phase)
    lhs, rhs = [], []
    for box in range(4):
        acc = None
        for c in range(K - 1, -1, -1):
            part = R[(c * 4 + box) * wide : (c * 4 + box + 1) * wide]
            if acc is None:
                acc = part
            else:
                low = jnp.where(zlane > 0, pltpu.roll(acc, 1, 1), 0.0)
                high = jnp.where(zlane < NZ - 1, pltpu.roll(acc, NZ - 1, 1), 0.0)
                acc = part + (low + high - 2.0 * acc)
        xb, yb = box // 2, box % 2
        if xb == 0:
            slot = nslots if yb == 0 else slots[(0, 1)]
            zrow = zone_ref[0:1] if yb == 0 else zhalo[slot][0:1]
        else:
            slot = jnp.int32(0)
            for off in range(-hops, hops + 1):
                if off != 0:
                    slot = jnp.where(side == off, slots[(off, yb)], slot)
            zrow = zhalo[slot][0:1]
        rhs.append(acc * qbuf[slot][2 * K : 2 * K + 1])
        owner = lax.broadcasted_iota(jnp.int32, (own * count, NZ), 0)
        number = lax.rem(owner, count) * own + owner // count
        lhs.append((number == jnp.broadcast_to(zrow, number.shape)).astype(jnp.float32))
    S = None
    for a, b in zip(lhs, rhs):
        part = lax.dot_general(
            a, b, (((1,), (1,)), ((), ())), precision=HIGHEST, preferred_element_type=jnp.float32
        )
        S = part if S is None else S + part
    pick = lax.broadcasted_iota(jnp.int32, (count, wide), 1) % own
    mine = S[:count]
    for zz in range(1, own):
        mine = jnp.where(pick == zz, S[zz * count : (zz + 1) * count], mine)
    mine = jnp.concatenate([mine, jnp.zeros((count, 128 - wide), jnp.float32)], axis=1)
    for o in range(count):
        sums[o] = mine[o : o + 1]

    def give(r, carry):
        peer = lax.rem(me + r, count)
        pltpu.make_async_remote_copy(
            src_ref=sums.at[peer],
            dst_ref=got.at[r - 1],
            send_sem=sum_send,
            recv_sem=sum_recv,
            device_id=where_is(peer // npen, peer % npen),
            device_id_type=MESH,
        ).start()
        return carry

    lax.fori_loop(1, count, give, 0)

    wait_halo(2)
    T = forward(1, start_ref, lambda T: None)
    for f in range(F):
        for p in range(depth):
            end_ref[f, p] = T[f][p]

    pltpu.make_async_copy(got, got, sum_recv).wait()
    pltpu.make_async_copy(got, got, sum_send).wait()
    total = sums[me] + jnp.sum(got[...], axis=0)
    for k in range(K):
        grad_ref[k : k + 1, :] = total[:, k * own : (k + 1) * own]


def solution(mesh):
    nslab, nsec, npen = mesh.shape["slab"], mesh.shape["section"], mesh.shape["pencil"]

    def per_device(check, start, target, zone, now, nxt, gain, diff, coup):
        F, depth, rows, NZ = check.shape
        K, zones = now.shape
        nline = nslab * nsec
        count = nline * npen
        hops = -(-K // depth)
        nslots = 2 * (2 * hops + 1) - 1
        table = jnp.asarray(geometry(nline * depth, npen * rows, depth, npen, K))
        cfg = (nslab, nsec, npen, F, depth, NZ, K, zones)
        vmem = pl.BlockSpec(memory_space=pltpu.VMEM)
        return pl.pallas_call(
            functools.partial(kernel, cfg),
            out_shape=(
                jax.ShapeDtypeStruct(check.shape, jnp.float32),
                jax.ShapeDtypeStruct((K, zones // count), jnp.float32),
            ),
            in_specs=[pl.BlockSpec(memory_space=pltpu.HBM)] * 10,
            out_specs=(vmem, vmem),
            scratch_shapes=[
                pltpu.VMEM(check.shape, jnp.float32),
                pltpu.VMEM(start.shape, jnp.float32),
                pltpu.VMEM(target.shape, jnp.float32),
                pltpu.VMEM((rows, NZ), jnp.int32),
                pltpu.VMEM(now.shape, jnp.float32),
                pltpu.VMEM(nxt.shape, jnp.float32),
                pltpu.VMEM(gain.shape, jnp.float32),
                pltpu.SMEM(diff.shape, jnp.float32),
                pltpu.SMEM(coup.shape, jnp.float32),
                pltpu.VMEM(table.shape[1:], jnp.float32),
                pltpu.VMEM((2, nslots, F, rows, NZ), jnp.float32),
                pltpu.VMEM((2, nslots, F, depth, rows, NZ), jnp.float32),
                pltpu.VMEM((2, nslots, F, rows, NZ), jnp.float32),
                pltpu.VMEM((nslots, rows, NZ), jnp.int32),
                pltpu.VMEM((nslots + 1, 2 * K + 8, NZ), jnp.float32),
                pltpu.VMEM((count, 1, 128), jnp.float32),
                pltpu.VMEM((count - 1, 1, 128), jnp.float32),
                pltpu.SemaphoreType.DMA((10,)),
                pltpu.SemaphoreType.DMA((3, nslots)),
                pltpu.SemaphoreType.DMA((3, nslots)),
                pltpu.SemaphoreType.DMA,
                pltpu.SemaphoreType.DMA,
            ],
            compiler_params=pltpu.CompilerParams(
                collective_id=0, has_side_effects=True, vmem_limit_bytes=32 * 1024 * 1024
            ),
        )(check, start, target, zone, now, nxt, gain, diff, coup, table)

    return jax.shard_map(
        per_device,
        mesh=mesh,
        in_specs=(
            P(None, ("scen", "slab", "section"), "pencil", None),
            P(None, ("scen", "slab", "section"), "pencil", None),
            P(("scen", "slab", "section"), "pencil", None),
            P(("scen", "slab", "section"), "pencil", None),
            P("scen", None),
            P("scen", None),
            P(),
            P(),
            P(),
        ),
        out_specs=(
            P(None, ("scen", "slab", "section"), "pencil", None),
            P("scen", ("slab", "section", "pencil")),
        ),
        check_vma=False,
    )
```

```python
import functools
import math

import jax
import jax.numpy as jnp
import numpy as np
from jax import lax
from jax.experimental import pallas as pl
from jax.experimental.pallas import tpu as pltpu
from jax.sharding import PartitionSpec as P

CELLS_ZONE = 1024
BOX = 8
HIGHEST = lax.Precision.HIGHEST
MESH = pl.DeviceIdType.MESH


def laplacian_1d(n):
    return -2.0 * np.eye(n) + np.eye(n, k=1) + np.eye(n, k=-1)


def geometry(nx, ny, depth, pencils, steps):
    rows = ny // pencils
    phases = BOX // depth
    lx, ly = laplacian_1d(nx), laplacian_1d(ny)
    boxes = nx // BOX

    def powers(bx, by):
        field = np.zeros((nx, ny))
        if 0 <= bx < boxes:
            field[bx * BOX : (bx + 1) * BOX, by * BOX : (by + 1) * BOX] = 1.0
        out = []
        for _ in range(steps):
            out.append(field)
            field = lx @ field + field @ ly.T
        return out

    table = np.zeros((phases * 3 * pencils, steps * 4, steps * depth * rows), np.float32)
    for phase in range(phases):
        side = -1 if 2 * phase < phases else 1
        for edge, bx in enumerate((0, boxes // 2, boxes - 1)):
            x0 = bx * BOX + phase * depth
            for pencil in range(pencils):
                for xb in range(2):
                    for yb in range(2):
                        fields = powers(bx + side * xb, pencil if yb == 0 else 1 - pencil)
                        for r in range(steps):
                            block = fields[r][x0 : x0 + depth, pencil * rows : (pencil + 1) * rows]
                            table[(phase * 3 + edge) * pencils + pencil, r * 4 + xb * 2 + yb] = (
                                np.tile(block.reshape(-1), steps)
                            )
    return table


def kernel(
    cfg,
    check_hbm,
    start_hbm,
    target_hbm,
    zone_hbm,
    now_hbm,
    next_hbm,
    gain_hbm,
    diff_hbm,
    coup_hbm,
    geo_hbm,
    end_ref,
    grad_ref,
    check_ref,
    start_ref,
    target_ref,
    zone_ref,
    now_ref,
    next_ref,
    gain_ref,
    diff_ref,
    coup_ref,
    geo_ref,
    packed,
    halo,
    corner,
    zhalo,
    qbuf,
    sums,
    got,
    load_sem,
    halo_send,
    halo_recv,
    sum_send,
    sum_recv,
):
    nslab, nsec, npen, F, depth, NZ, K, zones = cfg
    nline = nslab * nsec
    count = nline * npen
    own = zones // count
    hops = -(-K // depth)
    phases = BOX // depth
    pencil = lax.axis_index("pencil")
    line = lax.axis_index("slab") * nsec + lax.axis_index("section")
    me = line * npen + pencil
    phase = line % phases
    edge = jnp.where(line < phases, 0, jnp.where(line >= nline - phases, 2, 1))

    loads = [
        pltpu.make_async_copy(src, dst, load_sem.at[n])
        for n, (src, dst) in enumerate(
            (
                (check_hbm, check_ref),
                (start_hbm, start_ref),
                (coup_hbm, coup_ref),
                (diff_hbm, diff_ref),
                (geo_hbm.at[(phase * 3 + edge) * npen + pencil], geo_ref),
                (gain_hbm, gain_ref),
                (now_hbm, now_ref),
                (next_hbm, next_ref),
                (zone_hbm.at[0], zone_ref),
                (target_hbm, target_ref),
            )
        )
    ]
    for load in loads:
        load.start()

    def where_is(at, pen):
        return {"slab": at // nsec, "section": at % nsec, "pencil": pen}

    slots = {}
    for off in range(-hops, hops + 1):
        for other in range(2):
            if (off, other) != (0, 0):
                slots[(off, other)] = len(slots)
    nslots = len(slots)

    barrier = pltpu.get_barrier_semaphore()

    def greet(r, carry):
        peer = lax.rem(me + r, count)
        pl.semaphore_signal(
            barrier, inc=1, device_id=where_is(peer // npen, peer % npen), device_id_type=MESH
        )
        return carry

    lax.fori_loop(1, count, greet, 0)

    def exists(off):
        return jnp.logical_and(line + off >= 0, line + off < nline)

    for off, other in slots:
        if off != 0:
            slot = slots[(off, other)]

            @pl.when(jnp.logical_not(exists(off)))
            def _(slot=slot, other=other):
                for which in range(2):
                    if other:
                        corner[which, slot] = jnp.zeros_like(corner[which, slot])
                    else:
                        halo[which, slot] = jnp.zeros_like(halo[which, slot])
                zhalo[slot] = jnp.zeros_like(zhalo[slot])

    row = lax.broadcasted_iota(jnp.int32, (BOX, NZ), 0)

    def near(pen, at):
        return jnp.where(pen == 0, BOX - 1 - at, at)

    def turned(v, pen, back):
        first, second = (3, 5) if back else (5, 3)
        return jnp.where(pen == 0, pltpu.roll(v, first, 0), pltpu.roll(v, second, 0))

    near_1 = near(pencil, row) < 3
    near_2 = near(pencil, (row + 4) % BOX) < 2

    def plane_at(off, distance):
        plane = abs(off) * depth - distance
        plane = plane if off > 0 else depth - 1 - plane
        return plane if 0 <= plane < depth else None

    def pack(which, ref):
        for off in range(-hops, hops + 1):
            if off == 0:
                continue
            one, two, three = (plane_at(off, d) for d in (1, 2, 3))
            for f in range(F):
                tile = jnp.zeros((BOX, NZ), jnp.float32)
                if three is not None:
                    tile = turned(ref[f, three], pencil, False)
                if two is not None:
                    tile = jnp.where(near_2, pltpu.roll(ref[f, two], 4, 0), tile)
                if one is not None:
                    tile = jnp.where(near_1, ref[f, one], tile)
                packed[which, slots[(off, 1)], f] = tile

    loads[0].wait()
    pack(0, check_ref)
    loads[1].wait()
    pack(1, start_ref)
    pl.semaphore_wait(barrier, count - 1)

    def copy_to(what, off, other, arriving):
        here = slots[(off, other)]
        slot = here if arriving else slots[(-off, other)]
        if what == 0:
            src, dst = zone_hbm.at[0], zhalo.at[slot]
        elif off != 0 and other:
            src, dst = packed.at[what - 1, here], corner.at[what - 1, slot]
        else:
            src, dst = (check_hbm, start_hbm)[what - 1], halo.at[what - 1, slot]
        return pltpu.make_async_remote_copy(
            src_ref=src,
            dst_ref=dst,
            send_sem=halo_send.at[what, here],
            recv_sem=halo_recv.at[what, slot],
            device_id=where_is(line + off, pencil if other == 0 else 1 - pencil),
            device_id_type=MESH,
        )

    for what in range(3):
        for off, other in slots:

            @pl.when(exists(off))
            def _(off=off, other=other, what=what):
                copy_to(what, off, other, False).start()

    for load in loads[2:]:
        load.wait()

    diff = [diff_ref[f] for f in range(F)]
    coup = [[coup_ref[f, g] for g in range(F)] for f in range(F)]
    mix = [
        [coup[f][g] + (1.0 - 6.0 * diff[f]) if f == g else coup[f][g] for g in range(F)]
        for f in range(F)
    ]
    alpha = {(0, 0): jnp.float32(1.0)}
    rows = {0: [jnp.float32(1.0) if f == 0 else None for f in range(F)]}
    for p in range(1, K):
        new = {}
        for q in range(p + 1):
            vec = []
            for g in range(F):
                total = None
                if q in rows:
                    for f in range(F):
                        v = rows[q][f]
                        if v is not None:
                            c = coup[f][g] + 1.0 if f == g else coup[f][g]
                            total = v * c if total is None else total + v * c
                if q - 1 in rows and rows[q - 1][g] is not None:
                    v = rows[q - 1][g] * diff[g]
                    total = v if total is None else total + v
                vec.append(total)
            new[q] = vec
        rows = new
        for q in range(p + 1):
            alpha[(p, q)] = rows[q][0]

    lanes = K * depth * BOX
    wide = K * own
    shape = (wide, lanes)
    age = (
        lax.broadcasted_iota(jnp.int32, shape, 1) // (depth * BOX)
        - lax.broadcasted_iota(jnp.int32, shape, 0) // own
    )
    poly = []
    for q in range(K):
        part = jnp.zeros(shape, jnp.float32)
        for p in range(q, K):
            part = jnp.where(age == p, alpha[(p, q)], part)
        poly.append(part)
    geo = geo_ref[...]
    weights = []
    for c in range(K):
        for box in range(4):
            total = None
            for r in range(K - c):
                term = (math.comb(r + c, c) * poly[r + c]) * geo[r * 4 + box : r * 4 + box + 1]
                total = term if total is None else total + term
            weights.append(total)
    weights = jnp.concatenate(weights, axis=0)

    lane = lax.broadcasted_iota(jnp.int32, (BOX, NZ), 1)
    not_first, not_last = lane > 0, lane < NZ - 1
    top, bottom = row == BOX - 1, row == 0
    half = BOX // 2
    beyond = row // half == pencil

    def along_z(v):
        low = jnp.where(not_first[: v.shape[0]], pltpu.roll(v, 1, 1), 0.0)
        high = jnp.where(not_last[: v.shape[0]], pltpu.roll(v, NZ - 1, 1), 0.0)
        return low + high

    gain = gain_ref[...].reshape(1, zones)
    tables = jnp.concatenate(
        [
            now_ref[...] * gain,
            next_ref[...] * gain,
            jnp.broadcast_to(gain * (1.0 / math.sqrt(CELLS_ZONE)), (BOX, zones)),
        ],
        axis=0,
    )

    def inject(zrow, slot):
        zone = lax.broadcasted_iota(jnp.int32, (zones, NZ), 0)
        hot = (zone == jnp.broadcast_to(zrow, (zones, NZ))).astype(jnp.float32)
        qbuf[slot] = jnp.dot(tables, hot, precision=HIGHEST, preferred_element_type=jnp.float32)

    inject(zone_ref[0:1], nslots)

    for off, other in slots:

        @pl.when(exists(off))
        def _(off=off, other=other):
            copy = copy_to(0, off, other, True)
            copy.wait_send()
            copy.wait_recv()

    for off, other in slots:
        slot = slots[(off, other)]
        inject(zhalo[slot][0:1], slot)

    inside = {off: jnp.where(exists(off), 1.0, 0.0) for off in range(-hops, hops + 1)}

    def off_of(plane):
        return plane // depth

    def forward(which, ref, seen):
        def plane_of(f, plane, other):
            off = off_of(plane)
            if off == 0 and other == 0:
                return ref[f, plane]
            if off != 0 and other:
                v = corner[which, slots[(off, 1)], f]
                distance = -plane if off < 0 else plane - depth + 1
                if distance == 2:
                    v = pltpu.roll(v, 4, 0)
                if distance == 3:
                    v = turned(v, 1 - pencil, True)
                return jnp.where(near(1 - pencil, row) < K - distance, v, 0.0)
            v = halo[which, slots[(off, other)], f, plane - off * depth]
            return jnp.where(beyond, v, 0.0) if other else v

        T = [{p: plane_of(f, p, 0) for p in range(-K, depth + K)} for f in range(F)]
        U = [{p: plane_of(f, p, 1) for p in range(1 - K, depth + K - 1)} for f in range(F)]
        for step in range(K):
            reach = K - 1 - step
            newT = [{} for _ in range(F)]
            newU = [{} for _ in range(F)]
            for p in range(-reach, depth + reach):
                off = off_of(p)
                both = -reach < p < depth + reach - 1
                qt = qbuf[nslots if off == 0 else slots[(off, 0)], which * K + step : which * K + step + 1]
                if both:
                    qu = qbuf[slots[(off, 1)], which * K + step : which * K + step + 1]
                for f in range(F):
                    t, u = T[f][p], U[f][p]
                    tu, td = pltpu.roll(t, BOX - 1, 0), pltpu.roll(t, 1, 0)
                    uu, ud = pltpu.roll(u, BOX - 1, 0), pltpu.roll(u, 1, 0)
                    beside = T[f][p - 1] + T[f][p + 1] + along_z(t)
                    beside = beside + jnp.where(top, uu, tu) + jnp.where(bottom, ud, td)
                    v = diff[f] * beside
                    for g in range(F):
                        v = v + mix[f][g] * T[g][p]
                    if f == 0:
                        v = v + qt
                    if off != 0:
                        v = v * inside[off]
                    newT[f][p] = v
                    if both:
                        beside = U[f][p - 1] + U[f][p + 1] + along_z(u)
                        beside = beside + jnp.where(top, tu, uu) + jnp.where(bottom, td, ud)
                        v = diff[f] * beside
                        for g in range(F):
                            v = v + mix[f][g] * U[g][p]
                        if f == 0:
                            v = v + qu
                        if off != 0:
                            v = v * inside[off]
                        newU[f][p] = jnp.where(beyond, v, 0.0)
            T, U = newT, newU
            seen(T)
        return T

    def wait_halo(what):
        for off, other in slots:

            @pl.when(exists(off))
            def _(off=off, other=other):
                copy = copy_to(what, off, other, True)
                copy.wait_send()
                copy.wait_recv()

    wait_halo(1)
    misfits = []

    def seen(T):
        for p in range(depth):
            misfits.append(T[0][p] - target_ref[p])

    forward(0, check_ref, seen)
    R = jnp.dot(
        weights,
        jnp.concatenate(misfits, axis=0),
        precision=HIGHEST,
        preferred_element_type=jnp.float32,
    )
    zlane = lax.broadcasted_iota(jnp.int32, (wide, NZ), 1)
    side = jnp.where(2 * phase < phases, -(phase + 1), phases - phase)
    lhs, rhs = [], []
    for box in range(4):
        acc = None
        for c in range(K - 1, -1, -1):
            part = R[(c * 4 + box) * wide : (c * 4 + box + 1) * wide]
            if acc is None:
                acc = part
            else:
                low = jnp.where(zlane > 0, pltpu.roll(acc, 1, 1), 0.0)
                high = jnp.where(zlane < NZ - 1, pltpu.roll(acc, NZ - 1, 1), 0.0)
                acc = part + (low + high - 2.0 * acc)
        xb, yb = box // 2, box % 2
        if xb == 0:
            slot = nslots if yb == 0 else slots[(0, 1)]
            zrow = zone_ref[0:1] if yb == 0 else zhalo[slot][0:1]
        else:
            slot = jnp.int32(0)
            for off in range(-hops, hops + 1):
                if off != 0:
                    slot = jnp.where(side == off, slots[(off, yb)], slot)
            zrow = zhalo[slot][0:1]
        rhs.append(acc * qbuf[slot][2 * K : 2 * K + 1])
        owner = lax.broadcasted_iota(jnp.int32, (own * count, NZ), 0)
        number = lax.rem(owner, count) * own + owner // count
        lhs.append((number == jnp.broadcast_to(zrow, number.shape)).astype(jnp.float32))
    S = None
    for a, b in zip(lhs, rhs):
        part = lax.dot_general(
            a, b, (((1,), (1,)), ((), ())), precision=HIGHEST, preferred_element_type=jnp.float32
        )
        S = part if S is None else S + part
    pick = lax.broadcasted_iota(jnp.int32, (count, wide), 1) % own
    mine = S[:count]
    for zz in range(1, own):
        mine = jnp.where(pick == zz, S[zz * count : (zz + 1) * count], mine)
    mine = jnp.concatenate([mine, jnp.zeros((count, 128 - wide), jnp.float32)], axis=1)
    for o in range(count):
        sums[o] = mine[o : o + 1]

    def give(r, carry):
        peer = lax.rem(me + r, count)
        pltpu.make_async_remote_copy(
            src_ref=sums.at[peer],
            dst_ref=got.at[r - 1],
            send_sem=sum_send,
            recv_sem=sum_recv,
            device_id=where_is(peer // npen, peer % npen),
            device_id_type=MESH,
        ).start()
        return carry

    lax.fori_loop(1, count, give, 0)

    wait_halo(2)
    T = forward(1, start_ref, lambda T: None)
    for f in range(F):
        for p in range(depth):
            end_ref[f, p] = T[f][p]

    pltpu.make_async_copy(got, got, sum_recv).wait()
    pltpu.make_async_copy(got, got, sum_send).wait()
    total = sums[me] + jnp.sum(got[...], axis=0)
    for k in range(K):
        grad_ref[k : k + 1, :] = total[:, k * own : (k + 1) * own]


def solution(mesh):
    nslab, nsec, npen = mesh.shape["slab"], mesh.shape["section"], mesh.shape["pencil"]

    def per_device(check, start, target, zone, now, nxt, gain, diff, coup):
        F, depth, rows, NZ = check.shape
        K, zones = now.shape
        nline = nslab * nsec
        count = nline * npen
        hops = -(-K // depth)
        nslots = 2 * (2 * hops + 1) - 1
        table = jnp.asarray(geometry(nline * depth, npen * rows, depth, npen, K))
        cfg = (nslab, nsec, npen, F, depth, NZ, K, zones)
        vmem = pl.BlockSpec(memory_space=pltpu.VMEM)
        return pl.pallas_call(
            functools.partial(kernel, cfg),
            out_shape=(
                jax.ShapeDtypeStruct(check.shape, jnp.float32),
                jax.ShapeDtypeStruct((K, zones // count), jnp.float32),
            ),
            in_specs=[pl.BlockSpec(memory_space=pltpu.HBM)] * 10,
            out_specs=(vmem, vmem),
            scratch_shapes=[
                pltpu.VMEM(check.shape, jnp.float32),
                pltpu.VMEM(start.shape, jnp.float32),
                pltpu.VMEM(target.shape, jnp.float32),
                pltpu.VMEM((rows, NZ), jnp.int32),
                pltpu.VMEM(now.shape, jnp.float32),
                pltpu.VMEM(nxt.shape, jnp.float32),
                pltpu.VMEM(gain.shape, jnp.float32),
                pltpu.SMEM(diff.shape, jnp.float32),
                pltpu.SMEM(coup.shape, jnp.float32),
                pltpu.VMEM(table.shape[1:], jnp.float32),
                pltpu.VMEM((2, nslots, F, rows, NZ), jnp.float32),
                pltpu.VMEM((2, nslots, F, depth, rows, NZ), jnp.float32),
                pltpu.VMEM((2, nslots, F, rows, NZ), jnp.float32),
                pltpu.VMEM((nslots, rows, NZ), jnp.int32),
                pltpu.VMEM((nslots + 1, 2 * K + 8, NZ), jnp.float32),
                pltpu.VMEM((count, 1, 128), jnp.float32),
                pltpu.VMEM((count - 1, 1, 128), jnp.float32),
                pltpu.SemaphoreType.DMA((10,)),
                pltpu.SemaphoreType.DMA((3, nslots)),
                pltpu.SemaphoreType.DMA((3, nslots)),
                pltpu.SemaphoreType.DMA,
                pltpu.SemaphoreType.DMA,
            ],
            compiler_params=pltpu.CompilerParams(
                collective_id=0, has_side_effects=True, vmem_limit_bytes=62 * 1024 * 1024
            ),
        )(check, start, target, zone, now, nxt, gain, diff, coup, table)

    return jax.shard_map(
        per_device,
        mesh=mesh,
        in_specs=(
            P(None, ("scen", "slab", "section"), "pencil", None),
            P(None, ("scen", "slab", "section"), "pencil", None),
            P(("scen", "slab", "section"), "pencil", None),
            P(("scen", "slab", "section"), "pencil", None),
            P("scen", None),
            P("scen", None),
            P(),
            P(),
            P(),
        ),
        out_specs=(
            P(None, ("scen", "slab", "section"), "pencil", None),
            P("scen", ("slab", "section", "pencil")),
        ),
        check_vma=False,
    )
```

```python
import functools
import math

import jax
import jax.numpy as jnp
import numpy as np
from jax import lax
from jax.experimental import pallas as pl
from jax.experimental.pallas import tpu as pltpu
from jax.sharding import PartitionSpec as P

CELLS_ZONE = 1024
BOX = 8
HIGHEST = lax.Precision.HIGHEST
MESH = pl.DeviceIdType.MESH


def laplacian_1d(n):
    return -2.0 * np.eye(n) + np.eye(n, k=1) + np.eye(n, k=-1)


def geometry(nx, ny, depth, pencils, steps):
    rows = ny // pencils
    phases = BOX // depth
    lx, ly = laplacian_1d(nx), laplacian_1d(ny)
    boxes = nx // BOX

    def powers(bx, by):
        field = np.zeros((nx, ny))
        if 0 <= bx < boxes:
            field[bx * BOX : (bx + 1) * BOX, by * BOX : (by + 1) * BOX] = 1.0
        out = []
        for _ in range(steps):
            out.append(field)
            field = lx @ field + field @ ly.T
        return out

    table = np.zeros((phases * 3 * pencils, steps * 4, steps * depth * rows), np.float32)
    for phase in range(phases):
        side = -1 if 2 * phase < phases else 1
        for edge, bx in enumerate((0, boxes // 2, boxes - 1)):
            x0 = bx * BOX + phase * depth
            for pencil in range(pencils):
                for xb in range(2):
                    for yb in range(2):
                        fields = powers(bx + side * xb, pencil if yb == 0 else 1 - pencil)
                        for r in range(steps):
                            block = fields[r][x0 : x0 + depth, pencil * rows : (pencil + 1) * rows]
                            table[(phase * 3 + edge) * pencils + pencil, r * 4 + xb * 2 + yb] = (
                                np.tile(block.reshape(-1), steps)
                            )
    return table


def kernel(
    cfg,
    check_hbm,
    start_hbm,
    target_hbm,
    zone_hbm,
    now_hbm,
    next_hbm,
    gain_hbm,
    diff_hbm,
    coup_hbm,
    geo_hbm,
    end_ref,
    grad_ref,
    check_ref,
    start_ref,
    target_ref,
    zone_ref,
    now_ref,
    next_ref,
    gain_ref,
    diff_ref,
    coup_ref,
    geo_ref,
    packed,
    halo,
    corner,
    zhalo,
    qbuf,
    sums,
    got,
    load_sem,
    halo_send,
    halo_recv,
    ready,
    sum_send,
    sum_recv,
):
    nslab, nsec, npen, F, depth, NZ, K, zones = cfg
    nline = nslab * nsec
    count = nline * npen
    own = zones // count
    hops = -(-K // depth)
    phases = BOX // depth
    pencil = lax.axis_index("pencil")
    line = lax.axis_index("slab") * nsec + lax.axis_index("section")
    me = line * npen + pencil
    phase = line % phases
    edge = jnp.where(line < phases, 0, jnp.where(line >= nline - phases, 2, 1))

    loads = [
        pltpu.make_async_copy(src, dst, load_sem.at[n])
        for n, (src, dst) in enumerate(
            (
                (check_hbm, check_ref),
                (start_hbm, start_ref),
                (coup_hbm, coup_ref),
                (diff_hbm, diff_ref),
                (geo_hbm.at[(phase * 3 + edge) * npen + pencil], geo_ref),
                (gain_hbm, gain_ref),
                (now_hbm, now_ref),
                (next_hbm, next_ref),
                (zone_hbm.at[0], zone_ref),
                (target_hbm, target_ref),
            )
        )
    ]
    for load in loads:
        load.start()

    def where_is(at, pen):
        return {"slab": at // nsec, "section": at % nsec, "pencil": pen}

    slots = {}
    for off in range(-hops, hops + 1):
        for other in range(2):
            if (off, other) != (0, 0):
                slots[(off, other)] = len(slots)
    nslots = len(slots)

    barrier = pltpu.get_barrier_semaphore()

    def exists(off):
        return jnp.logical_and(line + off >= 0, line + off < nline)

    expected = 0
    for off, other in slots:
        expected = expected + exists(off).astype(jnp.int32)

        @pl.when(exists(off))
        def _(off=off, other=other):
            pl.semaphore_signal(
                barrier,
                inc=1,
                device_id=where_is(line + off, pencil if other == 0 else 1 - pencil),
                device_id_type=MESH,
            )

    strides = []
    reach = hops
    while reach < nline - 1:
        strides.append(reach)
        reach *= 2

    def tell(stage):
        for off in (-strides[stage], strides[stage]):

            @pl.when(exists(off))
            def _(off=off):
                pl.semaphore_signal(
                    ready.at[stage],
                    inc=1,
                    device_id=where_is(line + off, pencil),
                    device_id_type=MESH,
                )

    def hear(stage):
        far = strides[stage]
        pl.semaphore_wait(
            ready.at[stage], exists(-far).astype(jnp.int32) + exists(far).astype(jnp.int32)
        )

    for off, other in slots:
        if off != 0:
            slot = slots[(off, other)]

            @pl.when(jnp.logical_not(exists(off)))
            def _(slot=slot, other=other):
                for which in range(2):
                    if other:
                        corner[which, slot] = jnp.zeros_like(corner[which, slot])
                    else:
                        halo[which, slot] = jnp.zeros_like(halo[which, slot])
                zhalo[slot] = jnp.zeros_like(zhalo[slot])

    row = lax.broadcasted_iota(jnp.int32, (BOX, NZ), 0)

    def near(pen, at):
        return jnp.where(pen == 0, BOX - 1 - at, at)

    def turned(v, pen, back):
        first, second = (3, 5) if back else (5, 3)
        return jnp.where(pen == 0, pltpu.roll(v, first, 0), pltpu.roll(v, second, 0))

    near_1 = near(pencil, row) < 3
    near_2 = near(pencil, (row + 4) % BOX) < 2

    def plane_at(off, distance):
        plane = abs(off) * depth - distance
        plane = plane if off > 0 else depth - 1 - plane
        return plane if 0 <= plane < depth else None

    def pack(which, ref):
        for off in range(-hops, hops + 1):
            if off == 0:
                continue
            one, two, three = (plane_at(off, d) for d in (1, 2, 3))
            for f in range(F):
                tile = jnp.zeros((BOX, NZ), jnp.float32)
                if three is not None:
                    tile = turned(ref[f, three], pencil, False)
                if two is not None:
                    tile = jnp.where(near_2, pltpu.roll(ref[f, two], 4, 0), tile)
                if one is not None:
                    tile = jnp.where(near_1, ref[f, one], tile)
                packed[which, slots[(off, 1)], f] = tile

    loads[0].wait()
    pack(0, check_ref)
    loads[1].wait()
    pack(1, start_ref)
    pl.semaphore_wait(barrier, expected)
    if strides:
        tell(0)

    def copy_to(what, off, other, arriving):
        here = slots[(off, other)]
        slot = here if arriving else slots[(-off, other)]
        if what == 0:
            src, dst = zone_hbm.at[0], zhalo.at[slot]
        elif off != 0 and other:
            src, dst = packed.at[what - 1, here], corner.at[what - 1, slot]
        else:
            src, dst = (check_hbm, start_hbm)[what - 1], halo.at[what - 1, slot]
        return pltpu.make_async_remote_copy(
            src_ref=src,
            dst_ref=dst,
            send_sem=halo_send.at[what, here],
            recv_sem=halo_recv.at[what, slot],
            device_id=where_is(line + off, pencil if other == 0 else 1 - pencil),
            device_id_type=MESH,
        )

    for what in range(3):
        for off, other in slots:

            @pl.when(exists(off))
            def _(off=off, other=other, what=what):
                copy_to(what, off, other, False).start()

    for load in loads[2:]:
        load.wait()

    for stage in range(len(strides)):
        hear(stage)
        if stage + 1 < len(strides):
            tell(stage + 1)

    diff = [diff_ref[f] for f in range(F)]
    coup = [[coup_ref[f, g] for g in range(F)] for f in range(F)]
    mix = [
        [coup[f][g] + (1.0 - 6.0 * diff[f]) if f == g else coup[f][g] for g in range(F)]
        for f in range(F)
    ]
    alpha = {(0, 0): jnp.float32(1.0)}
    rows = {0: [jnp.float32(1.0) if f == 0 else None for f in range(F)]}
    for p in range(1, K):
        new = {}
        for q in range(p + 1):
            vec = []
            for g in range(F):
                total = None
                if q in rows:
                    for f in range(F):
                        v = rows[q][f]
                        if v is not None:
                            c = coup[f][g] + 1.0 if f == g else coup[f][g]
                            total = v * c if total is None else total + v * c
                if q - 1 in rows and rows[q - 1][g] is not None:
                    v = rows[q - 1][g] * diff[g]
                    total = v if total is None else total + v
                vec.append(total)
            new[q] = vec
        rows = new
        for q in range(p + 1):
            alpha[(p, q)] = rows[q][0]

    lanes = K * depth * BOX
    wide = K * own
    shape = (wide, lanes)
    age = (
        lax.broadcasted_iota(jnp.int32, shape, 1) // (depth * BOX)
        - lax.broadcasted_iota(jnp.int32, shape, 0) // own
    )
    poly = []
    for q in range(K):
        part = jnp.zeros(shape, jnp.float32)
        for p in range(q, K):
            part = jnp.where(age == p, alpha[(p, q)], part)
        poly.append(part)
    geo = geo_ref[...]
    weights = []
    for c in range(K):
        for box in range(4):
            total = None
            for r in range(K - c):
                term = (math.comb(r + c, c) * poly[r + c]) * geo[r * 4 + box : r * 4 + box + 1]
                total = term if total is None else total + term
            weights.append(total)
    weights = jnp.concatenate(weights, axis=0)

    lane = lax.broadcasted_iota(jnp.int32, (BOX, NZ), 1)
    not_first, not_last = lane > 0, lane < NZ - 1
    top, bottom = row == BOX - 1, row == 0
    half = BOX // 2
    beyond = row // half == pencil

    def along_z(v):
        low = jnp.where(not_first[: v.shape[0]], pltpu.roll(v, 1, 1), 0.0)
        high = jnp.where(not_last[: v.shape[0]], pltpu.roll(v, NZ - 1, 1), 0.0)
        return low + high

    gain = gain_ref[...].reshape(1, zones)
    tables = jnp.concatenate(
        [
            now_ref[...] * gain,
            next_ref[...] * gain,
            jnp.broadcast_to(gain * (1.0 / math.sqrt(CELLS_ZONE)), (BOX, zones)),
        ],
        axis=0,
    )

    def inject(zrow, slot):
        zone = lax.broadcasted_iota(jnp.int32, (zones, NZ), 0)
        hot = (zone == jnp.broadcast_to(zrow, (zones, NZ))).astype(jnp.float32)
        qbuf[slot] = jnp.dot(tables, hot, precision=HIGHEST, preferred_element_type=jnp.float32)

    inject(zone_ref[0:1], nslots)

    for off, other in slots:

        @pl.when(exists(off))
        def _(off=off, other=other):
            copy = copy_to(0, off, other, True)
            copy.wait_send()
            copy.wait_recv()

    for off, other in slots:
        slot = slots[(off, other)]
        inject(zhalo[slot][0:1], slot)

    inside = {off: jnp.where(exists(off), 1.0, 0.0) for off in range(-hops, hops + 1)}

    def off_of(plane):
        return plane // depth

    def forward(which, ref, seen):
        def plane_of(f, plane, other):
            off = off_of(plane)
            if off == 0 and other == 0:
                return ref[f, plane]
            if off != 0 and other:
                v = corner[which, slots[(off, 1)], f]
                distance = -plane if off < 0 else plane - depth + 1
                if distance == 2:
                    v = pltpu.roll(v, 4, 0)
                if distance == 3:
                    v = turned(v, 1 - pencil, True)
                return jnp.where(near(1 - pencil, row) < K - distance, v, 0.0)
            v = halo[which, slots[(off, other)], f, plane - off * depth]
            return jnp.where(beyond, v, 0.0) if other else v

        T = [{p: plane_of(f, p, 0) for p in range(-K, depth + K)} for f in range(F)]
        U = [{p: plane_of(f, p, 1) for p in range(1 - K, depth + K - 1)} for f in range(F)]
        for step in range(K):
            reach = K - 1 - step
            newT = [{} for _ in range(F)]
            newU = [{} for _ in range(F)]
            for p in range(-reach, depth + reach):
                off = off_of(p)
                both = -reach < p < depth + reach - 1
                qt = qbuf[nslots if off == 0 else slots[(off, 0)], which * K + step : which * K + step + 1]
                if both:
                    qu = qbuf[slots[(off, 1)], which * K + step : which * K + step + 1]
                for f in range(F):
                    t, u = T[f][p], U[f][p]
                    tu, td = pltpu.roll(t, BOX - 1, 0), pltpu.roll(t, 1, 0)
                    uu, ud = pltpu.roll(u, BOX - 1, 0), pltpu.roll(u, 1, 0)
                    beside = T[f][p - 1] + T[f][p + 1] + along_z(t)
                    beside = beside + jnp.where(top, uu, tu) + jnp.where(bottom, ud, td)
                    v = diff[f] * beside
                    for g in range(F):
                        v = v + mix[f][g] * T[g][p]
                    if f == 0:
                        v = v + qt
                    if off != 0:
                        v = v * inside[off]
                    newT[f][p] = v
                    if both:
                        beside = U[f][p - 1] + U[f][p + 1] + along_z(u)
                        beside = beside + jnp.where(top, tu, uu) + jnp.where(bottom, td, ud)
                        v = diff[f] * beside
                        for g in range(F):
                            v = v + mix[f][g] * U[g][p]
                        if f == 0:
                            v = v + qu
                        if off != 0:
                            v = v * inside[off]
                        newU[f][p] = jnp.where(beyond, v, 0.0)
            T, U = newT, newU
            seen(T)
        return T

    def wait_halo(what):
        for off, other in slots:

            @pl.when(exists(off))
            def _(off=off, other=other):
                copy = copy_to(what, off, other, True)
                copy.wait_send()
                copy.wait_recv()

    wait_halo(1)
    misfits = []

    def seen(T):
        for p in range(depth):
            misfits.append(T[0][p] - target_ref[p])

    forward(0, check_ref, seen)
    R = jnp.dot(
        weights,
        jnp.concatenate(misfits, axis=0),
        precision=HIGHEST,
        preferred_element_type=jnp.float32,
    )
    zlane = lax.broadcasted_iota(jnp.int32, (wide, NZ), 1)
    side = jnp.where(2 * phase < phases, -(phase + 1), phases - phase)
    lhs, rhs = [], []
    for box in range(4):
        acc = None
        for c in range(K - 1, -1, -1):
            part = R[(c * 4 + box) * wide : (c * 4 + box + 1) * wide]
            if acc is None:
                acc = part
            else:
                low = jnp.where(zlane > 0, pltpu.roll(acc, 1, 1), 0.0)
                high = jnp.where(zlane < NZ - 1, pltpu.roll(acc, NZ - 1, 1), 0.0)
                acc = part + (low + high - 2.0 * acc)
        xb, yb = box // 2, box % 2
        if xb == 0:
            slot = nslots if yb == 0 else slots[(0, 1)]
            zrow = zone_ref[0:1] if yb == 0 else zhalo[slot][0:1]
        else:
            slot = jnp.int32(0)
            for off in range(-hops, hops + 1):
                if off != 0:
                    slot = jnp.where(side == off, slots[(off, yb)], slot)
            zrow = zhalo[slot][0:1]
        rhs.append(acc * qbuf[slot][2 * K : 2 * K + 1])
        owner = lax.broadcasted_iota(jnp.int32, (own * count, NZ), 0)
        number = lax.rem(owner, count) * own + owner // count
        lhs.append((number == jnp.broadcast_to(zrow, number.shape)).astype(jnp.float32))
    S = None
    for a, b in zip(lhs, rhs):
        part = lax.dot_general(
            a, b, (((1,), (1,)), ((), ())), precision=HIGHEST, preferred_element_type=jnp.float32
        )
        S = part if S is None else S + part
    pick = lax.broadcasted_iota(jnp.int32, (count, wide), 1) % own
    mine = S[:count]
    for zz in range(1, own):
        mine = jnp.where(pick == zz, S[zz * count : (zz + 1) * count], mine)
    mine = jnp.concatenate([mine, jnp.zeros((count, 128 - wide), jnp.float32)], axis=1)
    for o in range(count):
        sums[o] = mine[o : o + 1]

    def give(r, carry):
        peer = lax.rem(me + r, count)
        pltpu.make_async_remote_copy(
            src_ref=sums.at[peer],
            dst_ref=got.at[r - 1],
            send_sem=sum_send,
            recv_sem=sum_recv,
            device_id=where_is(peer // npen, peer % npen),
            device_id_type=MESH,
        ).start()
        return carry

    lax.fori_loop(1, count, give, 0)

    wait_halo(2)
    T = forward(1, start_ref, lambda T: None)
    for f in range(F):
        for p in range(depth):
            end_ref[f, p] = T[f][p]

    pltpu.make_async_copy(got, got, sum_recv).wait()
    pltpu.make_async_copy(got, got, sum_send).wait()
    total = sums[me] + jnp.sum(got[...], axis=0)
    for k in range(K):
        grad_ref[k : k + 1, :] = total[:, k * own : (k + 1) * own]


def solution(mesh):
    nslab, nsec, npen = mesh.shape["slab"], mesh.shape["section"], mesh.shape["pencil"]

    def per_device(check, start, target, zone, now, nxt, gain, diff, coup):
        F, depth, rows, NZ = check.shape
        K, zones = now.shape
        nline = nslab * nsec
        count = nline * npen
        hops = -(-K // depth)
        nslots = 2 * (2 * hops + 1) - 1
        table = jnp.asarray(geometry(nline * depth, npen * rows, depth, npen, K))
        cfg = (nslab, nsec, npen, F, depth, NZ, K, zones)
        vmem = pl.BlockSpec(memory_space=pltpu.VMEM)
        return pl.pallas_call(
            functools.partial(kernel, cfg),
            out_shape=(
                jax.ShapeDtypeStruct(check.shape, jnp.float32),
                jax.ShapeDtypeStruct((K, zones // count), jnp.float32),
            ),
            in_specs=[pl.BlockSpec(memory_space=pltpu.HBM)] * 10,
            out_specs=(vmem, vmem),
            scratch_shapes=[
                pltpu.VMEM(check.shape, jnp.float32),
                pltpu.VMEM(start.shape, jnp.float32),
                pltpu.VMEM(target.shape, jnp.float32),
                pltpu.VMEM((rows, NZ), jnp.int32),
                pltpu.VMEM(now.shape, jnp.float32),
                pltpu.VMEM(nxt.shape, jnp.float32),
                pltpu.VMEM(gain.shape, jnp.float32),
                pltpu.SMEM(diff.shape, jnp.float32),
                pltpu.SMEM(coup.shape, jnp.float32),
                pltpu.VMEM(table.shape[1:], jnp.float32),
                pltpu.VMEM((2, nslots, F, rows, NZ), jnp.float32),
                pltpu.VMEM((2, nslots, F, depth, rows, NZ), jnp.float32),
                pltpu.VMEM((2, nslots, F, rows, NZ), jnp.float32),
                pltpu.VMEM((nslots, rows, NZ), jnp.int32),
                pltpu.VMEM((nslots + 1, 2 * K + 8, NZ), jnp.float32),
                pltpu.VMEM((count, 1, 128), jnp.float32),
                pltpu.VMEM((count - 1, 1, 128), jnp.float32),
                pltpu.SemaphoreType.DMA((10,)),
                pltpu.SemaphoreType.DMA((3, nslots)),
                pltpu.SemaphoreType.DMA((3, nslots)),
                pltpu.SemaphoreType.REGULAR((max(1, nline.bit_length()),)),
                pltpu.SemaphoreType.DMA,
                pltpu.SemaphoreType.DMA,
            ],
            compiler_params=pltpu.CompilerParams(
                collective_id=0, has_side_effects=True, vmem_limit_bytes=62 * 1024 * 1024
            ),
        )(check, start, target, zone, now, nxt, gain, diff, coup, table)

    return jax.shard_map(
        per_device,
        mesh=mesh,
        in_specs=(
            P(None, ("scen", "slab", "section"), "pencil", None),
            P(None, ("scen", "slab", "section"), "pencil", None),
            P(("scen", "slab", "section"), "pencil", None),
            P(("scen", "slab", "section"), "pencil", None),
            P("scen", None),
            P("scen", None),
            P(),
            P(),
            P(),
        ),
        out_specs=(
            P(None, ("scen", "slab", "section"), "pencil", None),
            P("scen", ("slab", "section", "pencil")),
        ),
        check_vma=False,
    )
```

```python
import functools
import math

import jax
import jax.numpy as jnp
import numpy as np
from jax import lax
from jax.experimental import pallas as pl
from jax.experimental.pallas import tpu as pltpu
from jax.sharding import PartitionSpec as P

CELLS_ZONE = 1024
BOX = 8
HIGHEST = lax.Precision.HIGHEST
MESH = pl.DeviceIdType.MESH


def laplacian_1d(n):
    return -2.0 * np.eye(n) + np.eye(n, k=1) + np.eye(n, k=-1)


def geometry(nx, ny, depth, pencils, steps):
    rows = ny // pencils
    phases = BOX // depth
    lx, ly = laplacian_1d(nx), laplacian_1d(ny)
    boxes = nx // BOX

    def powers(bx, by):
        field = np.zeros((nx, ny))
        if 0 <= bx < boxes:
            field[bx * BOX : (bx + 1) * BOX, by * BOX : (by + 1) * BOX] = 1.0
        out = []
        for _ in range(steps):
            out.append(field)
            field = lx @ field + field @ ly.T
        return out

    table = np.zeros((phases * 3 * pencils, steps * 4, steps * depth * rows), np.float32)
    for phase in range(phases):
        side = -1 if 2 * phase < phases else 1
        for edge, bx in enumerate((0, boxes // 2, boxes - 1)):
            x0 = bx * BOX + phase * depth
            for pencil in range(pencils):
                for xb in range(2):
                    for yb in range(2):
                        fields = powers(bx + side * xb, pencil if yb == 0 else 1 - pencil)
                        for r in range(steps):
                            block = fields[r][x0 : x0 + depth, pencil * rows : (pencil + 1) * rows]
                            table[(phase * 3 + edge) * pencils + pencil, r * 4 + xb * 2 + yb] = (
                                np.tile(block.reshape(-1), steps)
                            )
    return table


def kernel(
    cfg,
    check_hbm,
    start_hbm,
    target_hbm,
    zone_hbm,
    now_hbm,
    next_hbm,
    gain_hbm,
    diff_hbm,
    coup_hbm,
    geo_hbm,
    end_ref,
    grad_ref,
    check_ref,
    start_ref,
    target_ref,
    zone_ref,
    now_ref,
    next_ref,
    gain_ref,
    diff_ref,
    coup_ref,
    geo_ref,
    packed,
    halo,
    corner,
    zhalo,
    qbuf,
    sums,
    got,
    load_sem,
    halo_send,
    halo_recv,
    ready,
    sum_send,
    sum_recv,
):
    nslab, nsec, npen, F, depth, NZ, K, zones = cfg
    nline = nslab * nsec
    count = nline * npen
    own = zones // count
    hops = -(-K // depth)
    phases = BOX // depth
    pencil = lax.axis_index("pencil")
    line = lax.axis_index("slab") * nsec + lax.axis_index("section")
    me = line * npen + pencil
    phase = line % phases
    edge = jnp.where(line < phases, 0, jnp.where(line >= nline - phases, 2, 1))

    loads = [
        pltpu.make_async_copy(src, dst, load_sem.at[n])
        for n, (src, dst) in enumerate(
            (
                (check_hbm, check_ref),
                (start_hbm, start_ref),
                (coup_hbm, coup_ref),
                (diff_hbm, diff_ref),
                (geo_hbm.at[(phase * 3 + edge) * npen + pencil], geo_ref),
                (gain_hbm, gain_ref),
                (now_hbm, now_ref),
                (next_hbm, next_ref),
                (zone_hbm.at[0], zone_ref),
                (target_hbm, target_ref),
            )
        )
    ]
    for load in loads:
        load.start()

    def where_is(at, pen):
        return {"slab": at // nsec, "section": at % nsec, "pencil": pen}

    slots = {}
    for off in range(-hops, hops + 1):
        for other in range(2):
            if (off, other) != (0, 0):
                slots[(off, other)] = len(slots)
    nslots = len(slots)

    barrier = pltpu.get_barrier_semaphore()

    def exists(off):
        return jnp.logical_and(line + off >= 0, line + off < nline)

    expected = 0
    for off, other in slots:
        expected = expected + exists(off).astype(jnp.int32)

        @pl.when(exists(off))
        def _(off=off, other=other):
            pl.semaphore_signal(
                barrier,
                inc=1,
                device_id=where_is(line + off, pencil if other == 0 else 1 - pencil),
                device_id_type=MESH,
            )

    strides = []
    reach = hops
    while reach < nline - 1:
        strides.append(reach)
        reach *= 2

    def tell(stage):
        for off in (-strides[stage], strides[stage]):

            @pl.when(exists(off))
            def _(off=off):
                pl.semaphore_signal(
                    ready.at[stage],
                    inc=1,
                    device_id=where_is(line + off, pencil),
                    device_id_type=MESH,
                )

    def hear(stage):
        far = strides[stage]
        pl.semaphore_wait(
            ready.at[stage], exists(-far).astype(jnp.int32) + exists(far).astype(jnp.int32)
        )

    for off, other in slots:
        if off != 0:
            slot = slots[(off, other)]

            @pl.when(jnp.logical_not(exists(off)))
            def _(slot=slot, other=other):
                for which in range(2):
                    if other:
                        corner[which, slot] = jnp.zeros_like(corner[which, slot])
                    else:
                        halo[which, slot] = jnp.zeros_like(halo[which, slot])
                zhalo[slot] = jnp.zeros_like(zhalo[slot])

    for off in (-hops, hops):
        far = 0 if off < 0 else depth - 1
        if hops * depth == K:
            slot = slots[(off, 0)]
            halo[0, slot, 1:, far] = jnp.zeros((F - 1, BOX, NZ), jnp.float32)

    row = lax.broadcasted_iota(jnp.int32, (BOX, NZ), 0)

    def near(pen, at):
        return jnp.where(pen == 0, BOX - 1 - at, at)

    def turned(v, pen, back):
        first, second = (3, 5) if back else (5, 3)
        return jnp.where(pen == 0, pltpu.roll(v, first, 0), pltpu.roll(v, second, 0))

    near_1 = near(pencil, row) < 3
    near_2 = near(pencil, (row + 4) % BOX) < 2

    def plane_at(off, distance):
        plane = abs(off) * depth - distance
        plane = plane if off > 0 else depth - 1 - plane
        return plane if 0 <= plane < depth else None

    def pack(which, ref):
        for off in range(-hops, hops + 1):
            if off == 0:
                continue
            one, two, three = (plane_at(off, d) for d in (1, 2, 3))
            for f in range(F):
                tile = jnp.zeros((BOX, NZ), jnp.float32)
                if three is not None:
                    tile = turned(ref[f, three], pencil, False)
                if two is not None:
                    tile = jnp.where(near_2, pltpu.roll(ref[f, two], 4, 0), tile)
                if one is not None:
                    tile = jnp.where(near_1, ref[f, one], tile)
                packed[which, slots[(off, 1)], f] = tile

    loads[0].wait()
    pack(0, check_ref)
    loads[1].wait()
    pack(1, start_ref)
    pl.semaphore_wait(barrier, expected)
    if strides:
        tell(0)

    def copy_to(what, off, other, arriving):
        here = slots[(off, other)]
        slot = here if arriving else slots[(-off, other)]
        if what == 0:
            src, dst = zone_hbm.at[0], zhalo.at[slot]
        elif what == 3:
            far = plane_at(-off if arriving else off, K)
            src, dst = check_hbm.at[0, far], halo.at[0, slot, 0, far]
        elif what == 1 and not other and abs(off) == hops:
            planes = pl.ds(0 if plane_at(-off if arriving else off, K) else 1, depth - 1)
            src, dst = check_hbm.at[:, planes], halo.at[0, slot, :, planes]
        elif off != 0 and other:
            src, dst = packed.at[what - 1, here], corner.at[what - 1, slot]
        else:
            src, dst = (check_hbm, start_hbm)[what - 1], halo.at[what - 1, slot]
        return pltpu.make_async_remote_copy(
            src_ref=src,
            dst_ref=dst,
            send_sem=halo_send.at[what, here],
            recv_sem=halo_recv.at[what, slot],
            device_id=where_is(line + off, pencil if other == 0 else 1 - pencil),
            device_id_type=MESH,
        )

    def places(what):
        return [key for key in slots if what != 3 or (key[1] == 0 and abs(key[0]) == hops)]

    for what in (0, 1, 3, 2):
        for off, other in places(what):

            @pl.when(exists(off))
            def _(off=off, other=other, what=what):
                copy_to(what, off, other, False).start()

    for load in loads[2:]:
        load.wait()

    def pass_on(stages):
        for stage in stages:
            hear(stage)
            if stage + 1 < len(strides):
                tell(stage + 1)

    last = len(strides) - 1
    pass_on(range(min(1, last)))

    diff = [diff_ref[f] for f in range(F)]
    coup = [[coup_ref[f, g] for g in range(F)] for f in range(F)]
    mix = [
        [coup[f][g] + (1.0 - 6.0 * diff[f]) if f == g else coup[f][g] for g in range(F)]
        for f in range(F)
    ]
    alpha = {(0, 0): jnp.float32(1.0)}
    rows = {0: [jnp.float32(1.0) if f == 0 else None for f in range(F)]}
    for p in range(1, K):
        new = {}
        for q in range(p + 1):
            vec = []
            for g in range(F):
                total = None
                if q in rows:
                    for f in range(F):
                        v = rows[q][f]
                        if v is not None:
                            c = coup[f][g] + 1.0 if f == g else coup[f][g]
                            total = v * c if total is None else total + v * c
                if q - 1 in rows and rows[q - 1][g] is not None:
                    v = rows[q - 1][g] * diff[g]
                    total = v if total is None else total + v
                vec.append(total)
            new[q] = vec
        rows = new
        for q in range(p + 1):
            alpha[(p, q)] = rows[q][0]

    lanes = K * depth * BOX
    wide = K * own
    shape = (wide, lanes)
    age = (
        lax.broadcasted_iota(jnp.int32, shape, 1) // (depth * BOX)
        - lax.broadcasted_iota(jnp.int32, shape, 0) // own
    )
    poly = []
    for q in range(K):
        part = jnp.zeros(shape, jnp.float32)
        for p in range(q, K):
            part = jnp.where(age == p, alpha[(p, q)], part)
        poly.append(part)
    geo = geo_ref[...]
    weights = []
    for c in range(K):
        for box in range(4):
            total = None
            for r in range(K - c):
                term = (math.comb(r + c, c) * poly[r + c]) * geo[r * 4 + box : r * 4 + box + 1]
                total = term if total is None else total + term
            weights.append(total)
    weights = jnp.concatenate(weights, axis=0)

    lane = lax.broadcasted_iota(jnp.int32, (BOX, NZ), 1)
    not_first, not_last = lane > 0, lane < NZ - 1
    top, bottom = row == BOX - 1, row == 0
    half = BOX // 2
    beyond = row // half == pencil

    def along_z(v):
        low = jnp.where(not_first[: v.shape[0]], pltpu.roll(v, 1, 1), 0.0)
        high = jnp.where(not_last[: v.shape[0]], pltpu.roll(v, NZ - 1, 1), 0.0)
        return low + high

    gain = gain_ref[...].reshape(1, zones)
    tables = jnp.concatenate(
        [
            now_ref[...] * gain,
            next_ref[...] * gain,
            jnp.broadcast_to(gain * (1.0 / math.sqrt(CELLS_ZONE)), (BOX, zones)),
        ],
        axis=0,
    )

    def inject(zrow, slot):
        zone = lax.broadcasted_iota(jnp.int32, (zones, NZ), 0)
        hot = (zone == jnp.broadcast_to(zrow, (zones, NZ))).astype(jnp.float32)
        qbuf[slot] = jnp.dot(tables, hot, precision=HIGHEST, preferred_element_type=jnp.float32)

    inject(zone_ref[0:1], nslots)

    for off, other in slots:

        @pl.when(exists(off))
        def _(off=off, other=other):
            copy = copy_to(0, off, other, True)
            copy.wait_send()
            copy.wait_recv()

    for off, other in slots:
        slot = slots[(off, other)]
        inject(zhalo[slot][0:1], slot)
    pass_on(range(min(1, last), last))

    inside = {off: jnp.where(exists(off), 1.0, 0.0) for off in range(-hops, hops + 1)}

    def off_of(plane):
        return plane // depth

    def forward(which, ref, seen):
        def plane_of(f, plane, other):
            off = off_of(plane)
            if off == 0 and other == 0:
                return ref[f, plane]
            if off != 0 and other:
                v = corner[which, slots[(off, 1)], f]
                distance = -plane if off < 0 else plane - depth + 1
                if distance == 2:
                    v = pltpu.roll(v, 4, 0)
                if distance == 3:
                    v = turned(v, 1 - pencil, True)
                return jnp.where(near(1 - pencil, row) < K - distance, v, 0.0)
            v = halo[which, slots[(off, other)], f, plane - off * depth]
            return jnp.where(beyond, v, 0.0) if other else v

        T = [{p: plane_of(f, p, 0) for p in range(-K, depth + K)} for f in range(F)]
        U = [{p: plane_of(f, p, 1) for p in range(1 - K, depth + K - 1)} for f in range(F)]
        for step in range(K):
            reach = K - 1 - step
            newT = [{} for _ in range(F)]
            newU = [{} for _ in range(F)]
            for p in range(-reach, depth + reach):
                off = off_of(p)
                both = -reach < p < depth + reach - 1
                qt = qbuf[nslots if off == 0 else slots[(off, 0)], which * K + step : which * K + step + 1]
                if both:
                    qu = qbuf[slots[(off, 1)], which * K + step : which * K + step + 1]
                for f in range(F):
                    t, u = T[f][p], U[f][p]
                    tu, td = pltpu.roll(t, BOX - 1, 0), pltpu.roll(t, 1, 0)
                    uu, ud = pltpu.roll(u, BOX - 1, 0), pltpu.roll(u, 1, 0)
                    beside = T[f][p - 1] + T[f][p + 1] + along_z(t)
                    beside = beside + jnp.where(top, uu, tu) + jnp.where(bottom, ud, td)
                    v = diff[f] * beside
                    for g in range(F):
                        v = v + mix[f][g] * T[g][p]
                    if f == 0:
                        v = v + qt
                    if off != 0:
                        v = v * inside[off]
                    newT[f][p] = v
                    if both:
                        beside = U[f][p - 1] + U[f][p + 1] + along_z(u)
                        beside = beside + jnp.where(top, tu, uu) + jnp.where(bottom, td, ud)
                        v = diff[f] * beside
                        for g in range(F):
                            v = v + mix[f][g] * U[g][p]
                        if f == 0:
                            v = v + qu
                        if off != 0:
                            v = v * inside[off]
                        newU[f][p] = jnp.where(beyond, v, 0.0)
            T, U = newT, newU
            seen(T)
        return T

    def wait_halo(what):
        for off, other in places(what):

            @pl.when(exists(off))
            def _(off=off, other=other):
                copy = copy_to(what, off, other, True)
                copy.wait_send()
                copy.wait_recv()

    wait_halo(1)
    wait_halo(3)
    misfits = []

    def seen(T):
        for p in range(depth):
            misfits.append(T[0][p] - target_ref[p])

    forward(0, check_ref, seen)
    R = jnp.dot(
        weights,
        jnp.concatenate(misfits, axis=0),
        precision=HIGHEST,
        preferred_element_type=jnp.float32,
    )
    zlane = lax.broadcasted_iota(jnp.int32, (wide, NZ), 1)
    side = jnp.where(2 * phase < phases, -(phase + 1), phases - phase)
    lhs, rhs = [], []
    for box in range(4):
        acc = None
        for c in range(K - 1, -1, -1):
            part = R[(c * 4 + box) * wide : (c * 4 + box + 1) * wide]
            if acc is None:
                acc = part
            else:
                low = jnp.where(zlane > 0, pltpu.roll(acc, 1, 1), 0.0)
                high = jnp.where(zlane < NZ - 1, pltpu.roll(acc, NZ - 1, 1), 0.0)
                acc = part + (low + high - 2.0 * acc)
        xb, yb = box // 2, box % 2
        if xb == 0:
            slot = nslots if yb == 0 else slots[(0, 1)]
            zrow = zone_ref[0:1] if yb == 0 else zhalo[slot][0:1]
        else:
            slot = jnp.int32(0)
            for off in range(-hops, hops + 1):
                if off != 0:
                    slot = jnp.where(side == off, slots[(off, yb)], slot)
            zrow = zhalo[slot][0:1]
        rhs.append(acc * qbuf[slot][2 * K : 2 * K + 1])
        owner = lax.broadcasted_iota(jnp.int32, (own * count, NZ), 0)
        number = lax.rem(owner, count) * own + owner // count
        lhs.append((number == jnp.broadcast_to(zrow, number.shape)).astype(jnp.float32))
    S = None
    for a, b in zip(lhs, rhs):
        part = lax.dot_general(
            a, b, (((1,), (1,)), ((), ())), precision=HIGHEST, preferred_element_type=jnp.float32
        )
        S = part if S is None else S + part
    pick = lax.broadcasted_iota(jnp.int32, (count, wide), 1) % own
    mine = S[:count]
    for zz in range(1, own):
        mine = jnp.where(pick == zz, S[zz * count : (zz + 1) * count], mine)
    mine = jnp.concatenate([mine, jnp.zeros((count, 128 - wide), jnp.float32)], axis=1)
    for o in range(count):
        sums[o] = mine[o : o + 1]

    def give(r, carry):
        peer = lax.rem(me + r, count)
        pltpu.make_async_remote_copy(
            src_ref=sums.at[peer],
            dst_ref=got.at[r - 1],
            send_sem=sum_send,
            recv_sem=sum_recv,
            device_id=where_is(peer // npen, peer % npen),
            device_id_type=MESH,
        ).start()
        return carry

    pass_on(range(max(last, 0), last + 1))
    lax.fori_loop(1, count, give, 0)

    wait_halo(2)
    T = forward(1, start_ref, lambda T: None)
    for f in range(F):
        for p in range(depth):
            end_ref[f, p] = T[f][p]

    pltpu.make_async_copy(got, got, sum_recv).wait()
    pltpu.make_async_copy(got, got, sum_send).wait()
    total = sums[me] + jnp.sum(got[...], axis=0)
    for k in range(K):
        grad_ref[k : k + 1, :] = total[:, k * own : (k + 1) * own]


def solution(mesh):
    nslab, nsec, npen = mesh.shape["slab"], mesh.shape["section"], mesh.shape["pencil"]

    def per_device(check, start, target, zone, now, nxt, gain, diff, coup):
        F, depth, rows, NZ = check.shape
        K, zones = now.shape
        nline = nslab * nsec
        count = nline * npen
        hops = -(-K // depth)
        nslots = 2 * (2 * hops + 1) - 1
        table = jnp.asarray(geometry(nline * depth, npen * rows, depth, npen, K))
        cfg = (nslab, nsec, npen, F, depth, NZ, K, zones)
        vmem = pl.BlockSpec(memory_space=pltpu.VMEM)
        return pl.pallas_call(
            functools.partial(kernel, cfg),
            out_shape=(
                jax.ShapeDtypeStruct(check.shape, jnp.float32),
                jax.ShapeDtypeStruct((K, zones // count), jnp.float32),
            ),
            in_specs=[pl.BlockSpec(memory_space=pltpu.HBM)] * 10,
            out_specs=(vmem, vmem),
            scratch_shapes=[
                pltpu.VMEM(check.shape, jnp.float32),
                pltpu.VMEM(start.shape, jnp.float32),
                pltpu.VMEM(target.shape, jnp.float32),
                pltpu.VMEM((rows, NZ), jnp.int32),
                pltpu.VMEM(now.shape, jnp.float32),
                pltpu.VMEM(nxt.shape, jnp.float32),
                pltpu.VMEM(gain.shape, jnp.float32),
                pltpu.SMEM(diff.shape, jnp.float32),
                pltpu.SMEM(coup.shape, jnp.float32),
                pltpu.VMEM(table.shape[1:], jnp.float32),
                pltpu.VMEM((2, nslots, F, rows, NZ), jnp.float32),
                pltpu.VMEM((2, nslots, F, depth, rows, NZ), jnp.float32),
                pltpu.VMEM((2, nslots, F, rows, NZ), jnp.float32),
                pltpu.VMEM((nslots, rows, NZ), jnp.int32),
                pltpu.VMEM((nslots + 1, 2 * K + 8, NZ), jnp.float32),
                pltpu.VMEM((count, 1, 128), jnp.float32),
                pltpu.VMEM((count - 1, 1, 128), jnp.float32),
                pltpu.SemaphoreType.DMA((10,)),
                pltpu.SemaphoreType.DMA((4, nslots)),
                pltpu.SemaphoreType.DMA((4, nslots)),
                pltpu.SemaphoreType.REGULAR((max(1, nline.bit_length()),)),
                pltpu.SemaphoreType.DMA,
                pltpu.SemaphoreType.DMA,
            ],
            compiler_params=pltpu.CompilerParams(
                collective_id=0, has_side_effects=True, vmem_limit_bytes=62 * 1024 * 1024
            ),
        )(check, start, target, zone, now, nxt, gain, diff, coup, table)

    return jax.shard_map(
        per_device,
        mesh=mesh,
        in_specs=(
            P(None, ("scen", "slab", "section"), "pencil", None),
            P(None, ("scen", "slab", "section"), "pencil", None),
            P(("scen", "slab", "section"), "pencil", None),
            P(("scen", "slab", "section"), "pencil", None),
            P("scen", None),
            P("scen", None),
            P(),
            P(),
            P(),
        ),
        out_specs=(
            P(None, ("scen", "slab", "section"), "pencil", None),
            P("scen", ("slab", "section", "pencil")),
        ),
        check_vma=False,
    )
```
